32 devices in a mesh: ctx: 16 (over z, x, core), kvh: 2 (over y).
Axes of the slice: x: 2, y: 2, z: 4, core: 2. Of those that a mesh axis runs over, the one named last changes fastest.
Arguments:
- queries: bfloat16 [8192, 8192], P('ctx', 'kvh')
- key_vector_rows: bfloat16 [8192, 1024], P('ctx', 'kvh')
- value_vector_rows: bfloat16 [8192, 1024], P('ctx', 'kvh'), may hold values from -6 to 6
- block_picks: int32 [64, 8], P('ctx'), may hold values from 0 to 63, as said below
Outputs:
- attended: bfloat16 [8192, 8192], P(('ctx', 'kvh'))
The draws below stay inside these ranges and needn't reach their ends.
Inputs may be any that keep to these rules, and one draw needn't show every extreme that they name: block_picks[b, 0] = b. The other entries of a row name 7 distinct blocks that lie on other indices of ctx (block c lies on index c // 4). Over the 4 rows of one index of ctx, the entries naming blocks of any one other index are at most 2 and name at most 1 distinct blocks; both bounds are reached in every draw.
All inputs are finite; a program needn't handle non-finite values.
Results may differ from the reference program's by a relative error of at most 0.0047.
Values may be sent and summed in bfloat16 or wider, within the bound.
A program may use at most 64 MiB of HBM per device.

```python
import math
import jax
import jax.numpy as jnp
from jax import lax

H = 64
KEY_VALUE_HEADS = 8
HEAD_SIZE = 128
BLOCK_TOKENS = 128
PICKED_BLOCKS = 8
SEQUENCE_TOKENS = 8192
BPD = 4
SEQUENCE_BLOCKS = 64
QUERY_PER_GROUP = 8
REMOTE = 28
CAPD = 1
N_CTX = 16


def draw_key_vector_rows(key, part):
    renewed_key = jax.random.fold_in(key, 1)
    field_value = jnp.clip(jax.random.normal(renewed_key, (SEQUENCE_TOKENS, KEY_VALUE_HEADS, HEAD_SIZE), jnp.float32), -6.0, 6.0)
    return field_value.reshape(SEQUENCE_TOKENS, KEY_VALUE_HEADS * HEAD_SIZE).astype(jnp.bfloat16)


def draw_queries(key, part):
    renewed_key = jax.random.fold_in(key, 2)
    field_value = jnp.clip(jax.random.normal(renewed_key, (SEQUENCE_TOKENS, KEY_VALUE_HEADS, QUERY_PER_GROUP, HEAD_SIZE), jnp.float32), -6.0, 6.0)
    return field_value.reshape(SEQUENCE_TOKENS, H * HEAD_SIZE).astype(jnp.bfloat16)


def local_permutation(one_key):
    return jax.random.permutation(one_key, BPD)


def draw_block_picks(key, part):
    total_slots = (N_CTX - 1) * CAPD
    lowest = max(CAPD, REMOTE - total_slots)

    def one_device(device):
        device_key = jax.random.fold_in(key, device + 100)
        keys_five = jax.random.split(device_key, 5)
        others = (device + 1 + jax.random.permutation(keys_five[0], N_CTX - 1)) % N_CTX
        rest = CAPD + jax.random.permutation(keys_five[1], (N_CTX - 2) * CAPD)
        sequence = jnp.concatenate([jnp.arange(CAPD, dtype=jnp.int32), rest.astype(jnp.int32)])
        doubled = jax.random.randint(keys_five[2], (), lowest, REMOTE // 2 + 1)
        distinct_count = REMOTE - doubled
        positions = jnp.arange(REMOTE, dtype=jnp.int32)
        first_pass = sequence[jnp.minimum(positions, total_slots - 1)]
        second_pass = sequence[jnp.clip(positions - distinct_count, 0, total_slots - 1)]
        slot_ids = jnp.where(positions < distinct_count, first_pass, second_pass)
        owner_slot = slot_ids // CAPD
        copy_index = slot_ids % CAPD
        local_perms = jax.vmap(local_permutation)(jax.random.split(keys_five[3], N_CTX - 1))
        local_ids = local_perms[owner_slot, copy_index]
        block_ids = others[owner_slot] * BPD + local_ids
        grouped = block_ids.reshape(BPD, PICKED_BLOCKS - 1)[jax.random.permutation(keys_five[4], BPD)]
        diagonal = device * BPD + jnp.arange(BPD, dtype=jnp.int32)
        return jnp.concatenate([diagonal[:, None], grouped.astype(jnp.int32)], axis=1)
    rows_all = jax.vmap(one_device)(jnp.arange(N_CTX, dtype=jnp.int32))
    return rows_all.reshape(SEQUENCE_BLOCKS, PICKED_BLOCKS).astype(jnp.int32)


def block_levels(own_key, extent, pieces, least, largest):
    gain, own = 1.0, jax.random.fold_in(own_key, 6)
    for dim, shards_of in pieces:
        heights = jnp.exp(jax.random.uniform(jax.random.fold_in(own, dim), (shards_of,), jnp.float32, least / len(pieces), largest / len(pieces)))
        gain = gain * jnp.repeat(heights, extent[dim] // shards_of).reshape([-1 if axis == dim else 1 for axis in range(len(extent))])
    return gain


def normal_values(key, shape, width, bound, cuts=(), kind=jnp.bfloat16):
    result = jax.random.normal(key, shape, jnp.float32) * width
    if len(cuts) > 0:
        result = block_levels(key, shape, cuts, -0.22, 0.18) * result
    return jnp.clip(result, min=-bound, max=bound).astype(kind)


def setup_inputs(seed: int = 0) -> dict:
    key_list = jax.random.split(jax.random.key(seed), 5)
    return {
        "queries": draw_queries(jax.random.fold_in(key_list[4], 71), 0),
        "key_vector_rows": draw_key_vector_rows(jax.random.fold_in(key_list[4], 71), 0),
        "value_vector_rows": normal_values(key_list[2], (SEQUENCE_TOKENS, KEY_VALUE_HEADS * HEAD_SIZE), 1.0, 6.0, ((0, 16), (1, 2))),
        "block_picks": draw_block_picks(jax.random.fold_in(key_list[4], 71), 0),
    }


def reference(queries, key_vector_rows, value_vector_rows, block_picks):
    score_scale = 1.0 / math.sqrt(HEAD_SIZE)
    blocked_queries = queries.reshape(SEQUENCE_BLOCKS, BLOCK_TOKENS, KEY_VALUE_HEADS, QUERY_PER_GROUP, HEAD_SIZE)
    blocked_keys = key_vector_rows.reshape(SEQUENCE_BLOCKS, BLOCK_TOKENS, KEY_VALUE_HEADS, HEAD_SIZE)
    blocked_values = value_vector_rows.reshape(SEQUENCE_BLOCKS, BLOCK_TOKENS, KEY_VALUE_HEADS, HEAD_SIZE)
    positions = jnp.arange(BLOCK_TOKENS, dtype=jnp.int32)
    causal = positions[None, :] <= positions[:, None]
    visible = jnp.concatenate([causal, jnp.ones((BLOCK_TOKENS, (PICKED_BLOCKS - 1) * BLOCK_TOKENS), dtype=bool)], axis=1)

    def attend_one(pair):
        query_block, picked_row = pair
        key_selection = blocked_keys[picked_row].reshape(PICKED_BLOCKS * BLOCK_TOKENS, KEY_VALUE_HEADS, HEAD_SIZE).astype(jnp.float32)
        value_selection = blocked_values[picked_row].reshape(PICKED_BLOCKS * BLOCK_TOKENS, KEY_VALUE_HEADS, HEAD_SIZE).astype(jnp.float32)
        scores = jnp.einsum('qgxd,kgd->gxqk', query_block.astype(jnp.float32), key_selection) * score_scale
        scores = jnp.where(visible, scores, -jnp.inf)
        row_max = lax.optimization_barrier(jnp.max(scores, axis=-1, keepdims=True))
        exponents = jnp.exp(scores - row_max)
        totals = lax.optimization_barrier(jnp.sum(exponents, axis=-1, keepdims=True))
        weights = lax.optimization_barrier(exponents.astype(jnp.bfloat16)).astype(jnp.float32)
        blended = jnp.einsum('gxqk,kgd->qgxd', weights, value_selection)
        blended = blended / jnp.transpose(totals, (2, 0, 1, 3))
        return blended.reshape(BLOCK_TOKENS, H * HEAD_SIZE).astype(jnp.bfloat16)
    outputs = lax.map(attend_one, (blocked_queries, block_picks.astype(jnp.int32)))
    return outputs.reshape(SEQUENCE_TOKENS, H * HEAD_SIZE)
```

```python
import functools
import math

import jax
import jax.numpy as jnp
from jax import lax
from jax.experimental import pallas as pl
from jax.experimental.pallas import tpu as pltpu
from jax.sharding import PartitionSpec as P

HEAD_SIZE = 128
BLOCK_TOKENS = 128
MESH = pl.DeviceIdType.MESH


def attend_kernel(n, parts, groups, blocks, picked, width, *refs):
    (req_ref, picks_ref, q_hbm, k_ref, v_ref, out_ref), rest = refs[:6], refs[6:]
    stages, rest = rest[:groups], rest[groups:]
    recvs, rest = rest[:groups], rest[groups:]
    (
        asked,
        asked_smem,
        q_ref,
        o_ref,
        k_sel,
        v_sel,
        ask_send,
        ask_recv,
        kv_send,
        kv_recv,
        out_send,
        out_recv,
        local_sem,
    ) = rest
    me = lax.axis_index("ctx")
    part = lax.axis_index("kvh")
    part_rows = out_ref.shape[0]
    chunk = min(BLOCK_TOKENS, part_rows)
    part_chunks = part_rows // chunk
    block_chunks = BLOCK_TOKENS // chunk
    cols = groups * width

    q_copy = pltpu.make_async_copy(q_hbm, q_ref, local_sem.at[0])
    q_copy.start()

    barrier = pltpu.get_barrier_semaphore()

    def greet_ctx(d, _):
        peer = lax.rem(me + d, n)
        pl.semaphore_signal(barrier, inc=1, device_id=(peer, part), device_id_type=MESH)
        return 0

    def greet_kvh(d, _):
        peer = lax.rem(part + d, parts)
        pl.semaphore_signal(barrier, inc=1, device_id=(me, peer), device_id_type=MESH)
        return 0

    lax.fori_loop(1, n, greet_ctx, 0)
    lax.fori_loop(1, parts, greet_kvh, 0)
    pl.semaphore_wait(barrier, n - 1 + parts - 1)

    def ask_copy(d):
        peer = lax.rem(me + d, n)
        return pltpu.make_async_remote_copy(
            src_ref=req_ref.at[peer],
            dst_ref=asked.at[n - 1 - d],
            send_sem=ask_send.at[d - 1],
            recv_sem=ask_recv.at[n - 1 - d],
            device_id=(peer, part),
            device_id_type=MESH,
        )

    def kv_copy(g, d):
        peer = lax.rem(me + d, n)
        return pltpu.make_async_remote_copy(
            src_ref=stages[g].at[d - 1],
            dst_ref=recvs[g].at[n - 1 - d],
            send_sem=kv_send.at[g, d - 1],
            recv_sem=kv_recv.at[g, n - 1 - d],
            device_id=(peer, part),
            device_id_type=MESH,
        )

    def over_peers(action):
        def one(d, _):
            action(d)
            return 0

        lax.fori_loop(1, n, one, 0)

    over_peers(lambda d: ask_copy(d).start())
    v_sel[:, HEAD_SIZE:] = jnp.ones((picked * BLOCK_TOKENS, HEAD_SIZE), jnp.bfloat16)
    over_peers(lambda d: ask_copy(d).wait_recv())
    to_smem = pltpu.make_async_copy(asked, asked_smem, local_sem.at[1])
    to_smem.start()
    to_smem.wait()

    def send_group(g):
        lanes = slice(g * HEAD_SIZE, (g + 1) * HEAD_SIZE)

        def one(d):
            wanted = asked_smem[d - 1, 0, 0]
            stages[g][d - 1, :BLOCK_TOKENS, :] = k_ref[wanted, :, lanes]
            stages[g][d - 1, BLOCK_TOKENS:, :] = v_ref[wanted, :, lanes]
            kv_copy(g, d).start()

        over_peers(one)

    for g in range(min(2, groups)):
        send_group(g)
    q_copy.wait()

    scale = math.log2(math.e) / math.sqrt(HEAD_SIZE)
    first_block = lax.rem(part + 1, parts) * part_rows // BLOCK_TOKENS

    def out_remote(g, index):
        target = index // part_chunks
        row = pl.multiple_of(lax.rem(index, part_chunks) * chunk, chunk)
        col = pl.multiple_of(part * cols + g * width, HEAD_SIZE)
        src_row = pl.multiple_of(index * chunk, chunk)
        src_col = pl.multiple_of(g * width, HEAD_SIZE)
        src = o_ref.at[pl.ds(src_row, chunk), pl.ds(src_col, width)]
        dst = out_ref.at[pl.ds(row, chunk), pl.ds(col, width)]
        slot = part * part_chunks + lax.rem(index, part_chunks)
        remote = pltpu.make_async_remote_copy(
            src_ref=src,
            dst_ref=dst,
            send_sem=out_send.at[g, index],
            recv_sem=out_recv.at[g, slot],
            device_id=(me, target),
            device_id_type=MESH,
        )
        local = pltpu.make_async_copy(src, dst, out_send.at[g, index])
        return target, remote, local

    def step(t, _):
        g = t // blocks
        turn = lax.rem(t, blocks)
        b = lax.rem(first_block + turn, blocks)
        for gi in range(groups):

            @pl.when(jnp.logical_and(g == gi, turn == 0))
            def _():
                over_peers(lambda d: kv_copy(gi, d).wait_recv())
                if gi + 2 < groups:
                    send_group(gi + 2)

            @pl.when(g == gi)
            def _():
                lanes = slice(gi * HEAD_SIZE, (gi + 1) * HEAD_SIZE)
                k_sel[:BLOCK_TOKENS, :] = k_ref[b, :, lanes]
                v_sel[:BLOCK_TOKENS, :HEAD_SIZE] = v_ref[b, :, lanes]
                for j in range(1, picked):
                    owner = picks_ref[b, j] // blocks
                    slot = jnp.minimum(lax.rem(owner + (n - 1) - me, n), n - 2)
                    rows = slice(j * BLOCK_TOKENS, (j + 1) * BLOCK_TOKENS)
                    k_sel[rows, :] = recvs[gi][slot, :BLOCK_TOKENS, :]
                    v_sel[rows, :HEAD_SIZE] = recvs[gi][slot, BLOCK_TOKENS:, :]

        q_rows = pl.ds(pl.multiple_of(b * BLOCK_TOKENS, BLOCK_TOKENS), BLOCK_TOKENS)
        heads = width // HEAD_SIZE
        pair = 2 if heads % 2 == 0 else 1
        row_id = lax.broadcasted_iota(jnp.int32, (pair * BLOCK_TOKENS, BLOCK_TOKENS), 0)
        key_id = lax.broadcasted_iota(jnp.int32, (pair * BLOCK_TOKENS, BLOCK_TOKENS), 1)
        causal = key_id <= lax.rem(row_id, BLOCK_TOKENS)
        for h in range(0, heads, pair):
            lanes = [
                pl.ds(pl.multiple_of(g * width + (h + u) * HEAD_SIZE, HEAD_SIZE), HEAD_SIZE)
                for u in range(pair)
            ]
            q = jnp.concatenate([q_ref[q_rows, lane] for lane in lanes], axis=0)
            scores = lax.dot_general(
                q, k_sel[...], (((1,), (1,)), ((), ())), preferred_element_type=jnp.float32
            )
            own = jnp.where(causal, scores[:, :BLOCK_TOKENS], -jnp.inf)
            scores = jnp.concatenate([own, scores[:, BLOCK_TOKENS:]], axis=1)
            top = jnp.max(scores, axis=1, keepdims=True)
            weights = jnp.exp2((scores - top) * scale).astype(jnp.bfloat16)
            both = jnp.dot(weights, v_sel[...], preferred_element_type=jnp.float32)
            result = (both[:, :HEAD_SIZE] / both[:, HEAD_SIZE:]).astype(jnp.bfloat16)
            for u in range(pair):
                o_ref[q_rows, lanes[u]] = result[u * BLOCK_TOKENS : (u + 1) * BLOCK_TOKENS]
        for c in range(block_chunks):
            target, remote, local = out_remote(g, b * block_chunks + c)

            @pl.when(target != part)
            def _():
                remote.start()

            @pl.when(target == part)
            def _():
                local.start()

        return 0

    lax.fori_loop(0, groups * blocks, step, 0)

    def finish(t, _):
        g = t // (parts * part_chunks)
        index = lax.rem(t, parts * part_chunks)
        target, remote, local = out_remote(g, index)

        @pl.when(target != part)
        def _():
            remote.wait_send()
            row = pl.multiple_of(lax.rem(index, part_chunks) * chunk, chunk)
            col = pl.multiple_of(target * cols + g * width, HEAD_SIZE)
            landed = out_ref.at[pl.ds(row, chunk), pl.ds(col, width)]
            pltpu.make_async_remote_copy(
                src_ref=landed,
                dst_ref=landed,
                send_sem=out_send.at[g, index],
                recv_sem=out_recv.at[g, index],
                device_id=(me, target),
                device_id_type=MESH,
            ).wait_recv()

        @pl.when(target == part)
        def _():
            local.wait()

        return 0

    over_peers(lambda d: ask_copy(d).wait_send())
    for g in range(groups):
        over_peers(lambda d: kv_copy(g, d).wait_send())
    lax.fori_loop(0, groups * parts * part_chunks, finish, 0)


def body(queries, key_vector_rows, value_vector_rows, block_picks):
    n = lax.axis_size("ctx")
    parts = lax.axis_size("kvh")
    tokens, cols = queries.shape
    blocks = tokens // BLOCK_TOKENS
    picked = block_picks.shape[1]
    groups = key_vector_rows.shape[1] // HEAD_SIZE
    width = cols // groups
    keys = key_vector_rows.reshape(blocks, BLOCK_TOKENS, groups * HEAD_SIZE)
    values = value_vector_rows.reshape(blocks, BLOCK_TOKENS, groups * HEAD_SIZE)
    remote = block_picks[:, 1:].reshape(-1)
    owned = (remote // blocks)[None, :] == jnp.arange(n, dtype=jnp.int32)[:, None]
    wanted = jnp.max(jnp.where(owned, (remote % blocks)[None, :], 0), axis=1)
    wanted = jnp.broadcast_to(wanted[:, None, None], (n, 1, 128))

    vmem = pl.BlockSpec(memory_space=pltpu.VMEM)
    anywhere = pl.BlockSpec(memory_space=pl.ANY)
    part_rows = tokens // parts
    chunks = tokens // min(BLOCK_TOKENS, part_rows)
    slots = pltpu.VMEM((n - 1, 2 * BLOCK_TOKENS, HEAD_SIZE), jnp.bfloat16)
    return pl.pallas_call(
        functools.partial(attend_kernel, n, parts, groups, blocks, picked, width),
        out_shape=jax.ShapeDtypeStruct((part_rows, parts * cols), jnp.bfloat16),
        in_specs=[vmem, pl.BlockSpec(memory_space=pltpu.SMEM), anywhere, vmem, vmem],
        out_specs=anywhere,
        scratch_shapes=[slots] * (2 * groups)
        + [
            pltpu.VMEM((n - 1, 1, 128), jnp.int32),
            pltpu.SMEM((n - 1, 1, 128), jnp.int32),
            pltpu.VMEM((tokens, cols), jnp.bfloat16),
            pltpu.VMEM((tokens, cols), jnp.bfloat16),
            pltpu.VMEM((picked * BLOCK_TOKENS, HEAD_SIZE), jnp.bfloat16),
            pltpu.VMEM((picked * BLOCK_TOKENS, 2 * HEAD_SIZE), jnp.bfloat16),
            pltpu.SemaphoreType.DMA((n - 1,)),
            pltpu.SemaphoreType.DMA((n - 1,)),
            pltpu.SemaphoreType.DMA((groups, n - 1)),
            pltpu.SemaphoreType.DMA((groups, n - 1)),
            pltpu.SemaphoreType.DMA((groups, chunks)),
            pltpu.SemaphoreType.DMA((groups, chunks)),
            pltpu.SemaphoreType.DMA((2,)),
        ],
        compiler_params=pltpu.CompilerParams(
            collective_id=0, has_side_effects=True, vmem_limit_bytes=48 * 2**20
        ),
        cost_estimate=pl.CostEstimate(
            flops=4 * tokens * cols * picked * BLOCK_TOKENS,
            bytes_accessed=4 * tokens * cols,
            transcendentals=tokens * (cols // HEAD_SIZE) * picked * BLOCK_TOKENS,
        ),
    )(wanted, block_picks, queries, keys, values)


def solution(mesh):
    return jax.shard_map(
        body,
        mesh=mesh,
        in_specs=(P("ctx", "kvh"), P("ctx", "kvh"), P("ctx", "kvh"), P("ctx", None)),
        out_specs=P(("ctx", "kvh"), None),
        check_vma=False,
    )
```

```python
import functools
import math

import jax
import jax.numpy as jnp
from jax import lax
from jax.experimental import pallas as pl
from jax.experimental.pallas import tpu as pltpu
from jax.sharding import PartitionSpec as P

HEAD_SIZE = 128
BLOCK_TOKENS = 128
MESH = pl.DeviceIdType.MESH


def attend_kernel(n, line, parts, groups, blocks, picked, width, *refs):
    (req_ref, picks_ref, q_hbm, k_ref, v_ref, out_ref), rest = refs[:6], refs[6:]
    owns, rest = rest[:groups], rest[groups:]
    from_left, rest = rest[: groups * (line - 1)], rest[groups * (line - 1) :]
    from_right, rest = rest[: groups * (line - 1)], rest[groups * (line - 1) :]
    stages, rest = rest[:groups], rest[groups:]
    chosen, rest = rest[:groups], rest[groups:]
    (
        asked,
        asked_smem,
        q_ref,
        o_ref,
        k_sel,
        v_sel,
        ask_send,
        ask_recv,
        right_send,
        left_recv,
        left_send,
        right_recv,
        plane_send,
        plane_recv,
        out_send,
        out_recv,
        local_sem,
    ) = rest
    me = lax.axis_index("ctx")
    part = lax.axis_index("kvh")
    plane = n // line
    place, seat = me // plane, lax.rem(me, plane)
    part_rows = out_ref.shape[0]
    chunk = min(BLOCK_TOKENS, part_rows)
    part_chunks = part_rows // chunk
    block_chunks = BLOCK_TOKENS // chunk
    cols = groups * width

    q_copy = pltpu.make_async_copy(q_hbm, q_ref, local_sem.at[0])
    q_copy.start()

    barrier = pltpu.get_barrier_semaphore()

    def greet_ctx(d, _):
        peer = lax.rem(me + d, n)
        pl.semaphore_signal(barrier, inc=1, device_id=(peer, part), device_id_type=MESH)
        return 0

    def greet_kvh(d, _):
        peer = lax.rem(part + d, parts)
        pl.semaphore_signal(barrier, inc=1, device_id=(me, peer), device_id_type=MESH)
        return 0

    lax.fori_loop(1, n, greet_ctx, 0)
    lax.fori_loop(1, parts, greet_kvh, 0)

    def pack(g):
        lanes = slice(g * HEAD_SIZE, (g + 1) * HEAD_SIZE)
        for i in range(blocks):
            owns[g][i, :BLOCK_TOKENS, :] = k_ref[i, :, lanes]
            owns[g][i, BLOCK_TOKENS:, :] = v_ref[i, :, lanes]

    for g in range(groups):
        pack(g)
    asked[plane - 1] = req_ref[...]
    v_sel[:, HEAD_SIZE:] = jnp.ones((picked * BLOCK_TOKENS, HEAD_SIZE), jnp.bfloat16)
    pl.semaphore_wait(barrier, n - 1 + parts - 1)

    def over_peers(action):
        def one(d, _):
            action(d)
            return 0

        lax.fori_loop(1, plane, one, 0)

    def plane_peer(d):
        return (place * plane + lax.rem(seat + d, plane), part)

    def ask_copy(d):
        return pltpu.make_async_remote_copy(
            src_ref=req_ref,
            dst_ref=asked.at[plane - 1 - d],
            send_sem=ask_send.at[d - 1],
            recv_sem=ask_recv.at[plane - 1 - d],
            device_id=plane_peer(d),
            device_id_type=MESH,
        )

    def right_copy(g, k):
        return pltpu.make_async_remote_copy(
            src_ref=owns[g] if k == 0 else from_left[g * (line - 1) + k - 1],
            dst_ref=from_left[g * (line - 1) + k],
            send_sem=right_send.at[g, k],
            recv_sem=left_recv.at[g, k],
            device_id=(me + plane, part),
            device_id_type=MESH,
        )

    def left_copy(g, k):
        return pltpu.make_async_remote_copy(
            src_ref=owns[g] if k == 0 else from_right[g * (line - 1) + k - 1],
            dst_ref=from_right[g * (line - 1) + k],
            send_sem=left_send.at[g, k],
            recv_sem=right_recv.at[g, k],
            device_id=(me - plane, part),
            device_id_type=MESH,
        )

    def plane_copy(g, d, source):
        return pltpu.make_async_remote_copy(
            src_ref=stages[g].at[d - 1, source],
            dst_ref=chosen[g].at[plane - 1 - d, source],
            send_sem=plane_send.at[g, d - 1, source],
            recv_sem=plane_recv.at[g, plane - 1 - d, source],
            device_id=plane_peer(d),
            device_id_type=MESH,
        )

    def share(g, shard, source):
        owner = source * plane + seat

        def one(d):
            wanted = asked_smem[d - 1, 0, owner]
            stages[g][d - 1, source] = shard[wanted]
            plane_copy(g, d, source).start()

        over_peers(one)
        chosen[g][plane - 1, source] = shard[asked_smem[plane - 1, 0, owner]]

    def begin(g):
        @pl.when(place < line - 1)
        def _():
            right_copy(g, 0).start()

        @pl.when(place > 0)
        def _():
            left_copy(g, 0).start()

    def hop(g, k):
        last = line - 1

        @pl.when(place >= k)
        def _():
            right_copy(g, k - 1).wait_recv()
            if k < last:

                @pl.when(place < last)
                def _():
                    right_copy(g, k).start()

        @pl.when(place + k <= last)
        def _():
            left_copy(g, k - 1).wait_recv()
            if k < last:

                @pl.when(place > 0)
                def _():
                    left_copy(g, k).start()

        if k == 1 and g + 1 < groups:
            begin(g + 1)
            share(g + 1, owns[g + 1], place)

        @pl.when(place >= k)
        def _():
            share(g, from_left[g * (line - 1) + k - 1], place - k)

        @pl.when(place + k <= last)
        def _():
            share(g, from_right[g * (line - 1) + k - 1], place + k)

    def wait_chosen(g):
        def one(d):
            def source(i, _):
                plane_copy(g, d, i).wait_recv()
                return 0

            lax.fori_loop(0, line, source, 0)

        over_peers(one)

    over_peers(lambda d: ask_copy(d).start())
    begin(0)
    over_peers(lambda d: ask_copy(d).wait_recv())
    to_smem = pltpu.make_async_copy(asked, asked_smem, local_sem.at[1])
    to_smem.start()
    to_smem.wait()
    share(0, owns[0], place)
    for k in range(1, line):
        hop(0, k)
    q_copy.wait()

    scale = math.log2(math.e) / math.sqrt(HEAD_SIZE)
    first_block = lax.rem(part + 1, parts) * part_rows // BLOCK_TOKENS

    def out_remote(g, index):
        target = index // part_chunks
        row = pl.multiple_of(lax.rem(index, part_chunks) * chunk, chunk)
        col = pl.multiple_of(part * cols + g * width, HEAD_SIZE)
        src_row = pl.multiple_of(index * chunk, chunk)
        src_col = pl.multiple_of(g * width, HEAD_SIZE)
        src = o_ref.at[pl.ds(src_row, chunk), pl.ds(src_col, width)]
        dst = out_ref.at[pl.ds(row, chunk), pl.ds(col, width)]
        slot = part * part_chunks + lax.rem(index, part_chunks)
        remote = pltpu.make_async_remote_copy(
            src_ref=src,
            dst_ref=dst,
            send_sem=out_send.at[g, index],
            recv_sem=out_recv.at[g, slot],
            device_id=(me, target),
            device_id_type=MESH,
        )
        local = pltpu.make_async_copy(src, dst, out_send.at[g, index])
        return target, remote, local

    hop_turn = {k: (k - 1) * blocks // (line - 1) + (1 if k > 1 else 0) for k in range(1, line)}
    hop_turn = {k: min(turn, blocks - 1) for k, turn in hop_turn.items()}

    def step(t, _):
        g = t // blocks
        turn = lax.rem(t, blocks)
        b = lax.rem(first_block + turn, blocks)
        for gi in range(groups):
            for ti in range(blocks):
                hops = [k for k in range(1, line) if hop_turn[k] == ti and gi + 1 < groups]
                if not hops and ti > 0:
                    continue

                @pl.when(jnp.logical_and(g == gi, turn == ti))
                def _():
                    for k in hops:
                        hop(gi + 1, k)
                    if ti == 0:
                        wait_chosen(gi)

            @pl.when(g == gi)
            def _():
                lanes = slice(gi * HEAD_SIZE, (gi + 1) * HEAD_SIZE)
                k_sel[:BLOCK_TOKENS, :] = k_ref[b, :, lanes]
                v_sel[:BLOCK_TOKENS, :HEAD_SIZE] = v_ref[b, :, lanes]
                for j in range(1, picked):
                    owner = picks_ref[b, j] // blocks
                    slot = lax.rem(lax.rem(owner, plane) + (plane - 1) - seat + plane, plane)
                    rows = slice(j * BLOCK_TOKENS, (j + 1) * BLOCK_TOKENS)
                    k_sel[rows, :] = chosen[gi][slot, owner // plane, :BLOCK_TOKENS, :]
                    v_sel[rows, :HEAD_SIZE] = chosen[gi][slot, owner // plane, BLOCK_TOKENS:, :]

        q_rows = pl.ds(pl.multiple_of(b * BLOCK_TOKENS, BLOCK_TOKENS), BLOCK_TOKENS)
        heads = width // HEAD_SIZE
        pair = 2 if heads % 2 == 0 else 1
        row_id = lax.broadcasted_iota(jnp.int32, (pair * BLOCK_TOKENS, BLOCK_TOKENS), 0)
        key_id = lax.broadcasted_iota(jnp.int32, (pair * BLOCK_TOKENS, BLOCK_TOKENS), 1)
        causal = key_id <= lax.rem(row_id, BLOCK_TOKENS)
        for h in range(0, heads, pair):
            lanes = [
                pl.ds(pl.multiple_of(g * width + (h + u) * HEAD_SIZE, HEAD_SIZE), HEAD_SIZE)
                for u in range(pair)
            ]
            q = jnp.concatenate([q_ref[q_rows, lane] for lane in lanes], axis=0)
            scores = lax.dot_general(
                q, k_sel[...], (((1,), (1,)), ((), ())), preferred_element_type=jnp.float32
            )
            own = jnp.where(causal, scores[:, :BLOCK_TOKENS], -jnp.inf)
            scores = jnp.concatenate([own, scores[:, BLOCK_TOKENS:]], axis=1)
            top = jnp.max(scores, axis=1, keepdims=True)
            weights = jnp.exp2((scores - top) * scale).astype(jnp.bfloat16)
            both = jnp.dot(weights, v_sel[...], preferred_element_type=jnp.float32)
            result = (both[:, :HEAD_SIZE] / both[:, HEAD_SIZE:]).astype(jnp.bfloat16)
            for u in range(pair):
                o_ref[q_rows, lanes[u]] = result[u * BLOCK_TOKENS : (u + 1) * BLOCK_TOKENS]
        for c in range(block_chunks):
            target, remote, local = out_remote(g, b * block_chunks + c)

            @pl.when(target != part)
            def _():
                remote.start()

            @pl.when(target == part)
            def _():
                local.start()

        return 0

    lax.fori_loop(0, groups * blocks, step, 0)

    def finish(t, _):
        g = t // (parts * part_chunks)
        index = lax.rem(t, parts * part_chunks)
        target, remote, local = out_remote(g, index)

        @pl.when(target != part)
        def _():
            remote.wait_send()
            row = pl.multiple_of(lax.rem(index, part_chunks) * chunk, chunk)
            col = pl.multiple_of(target * cols + g * width, HEAD_SIZE)
            landed = out_ref.at[pl.ds(row, chunk), pl.ds(col, width)]
            pltpu.make_async_remote_copy(
                src_ref=landed,
                dst_ref=landed,
                send_sem=out_send.at[g, index],
                recv_sem=out_recv.at[g, index],
                device_id=(me, target),
                device_id_type=MESH,
            ).wait_recv()

        @pl.when(target == part)
        def _():
            local.wait()

        return 0

    def plane_done(d):
        for g in range(groups):

            def source(i, _):
                plane_copy(g, d, i).wait_send()
                return 0

            lax.fori_loop(0, line, source, 0)

    over_peers(lambda d: ask_copy(d).wait_send())
    over_peers(plane_done)
    for g in range(groups):
        for k in range(line - 1):

            @pl.when(jnp.logical_and(place < line - 1, place >= k))
            def _():
                right_copy(g, k).wait_send()

            @pl.when(jnp.logical_and(place > 0, place + k <= line - 1))
            def _():
                left_copy(g, k).wait_send()

    lax.fori_loop(0, groups * parts * part_chunks, finish, 0)


def body(line, queries, key_vector_rows, value_vector_rows, block_picks):
    n = lax.axis_size("ctx")
    parts = lax.axis_size("kvh")
    tokens, cols = queries.shape
    blocks = tokens // BLOCK_TOKENS
    picked = block_picks.shape[1]
    groups = key_vector_rows.shape[1] // HEAD_SIZE
    width = cols // groups
    keys = key_vector_rows.reshape(blocks, BLOCK_TOKENS, groups * HEAD_SIZE)
    values = value_vector_rows.reshape(blocks, BLOCK_TOKENS, groups * HEAD_SIZE)
    remote = block_picks[:, 1:].reshape(-1)
    owned = (remote // blocks)[None, :] == jnp.arange(n, dtype=jnp.int32)[:, None]
    wanted = jnp.max(jnp.where(owned, (remote % blocks)[None, :], 0), axis=1)
    lanes = -(-n // 128) * 128
    wanted = jnp.pad(wanted, (0, lanes - n)).reshape(1, lanes)

    vmem = pl.BlockSpec(memory_space=pltpu.VMEM)
    anywhere = pl.BlockSpec(memory_space=pl.ANY)
    part_rows = tokens // parts
    chunks = tokens // min(BLOCK_TOKENS, part_rows)
    plane = n // line
    shard = pltpu.VMEM((blocks, 2 * BLOCK_TOKENS, HEAD_SIZE), jnp.bfloat16)
    stage = pltpu.VMEM((plane - 1, line, 2 * BLOCK_TOKENS, HEAD_SIZE), jnp.bfloat16)
    slots = pltpu.VMEM((plane, line, 2 * BLOCK_TOKENS, HEAD_SIZE), jnp.bfloat16)
    return pl.pallas_call(
        functools.partial(attend_kernel, n, line, parts, groups, blocks, picked, width),
        out_shape=jax.ShapeDtypeStruct((part_rows, parts * cols), jnp.bfloat16),
        in_specs=[vmem, pl.BlockSpec(memory_space=pltpu.SMEM), anywhere, vmem, vmem],
        out_specs=anywhere,
        scratch_shapes=[shard] * (groups * (2 * line - 1))
        + [stage] * groups
        + [slots] * groups
        + [
            pltpu.VMEM((plane, 1, lanes), jnp.int32),
            pltpu.SMEM((plane, 1, lanes), jnp.int32),
            pltpu.VMEM((tokens, cols), jnp.bfloat16),
            pltpu.VMEM((tokens, cols), jnp.bfloat16),
            pltpu.VMEM((picked * BLOCK_TOKENS, HEAD_SIZE), jnp.bfloat16),
            pltpu.VMEM((picked * BLOCK_TOKENS, 2 * HEAD_SIZE), jnp.bfloat16),
            pltpu.SemaphoreType.DMA((plane - 1,)),
            pltpu.SemaphoreType.DMA((plane - 1,)),
            pltpu.SemaphoreType.DMA((groups, line)),
            pltpu.SemaphoreType.DMA((groups, line)),
            pltpu.SemaphoreType.DMA((groups, line)),
            pltpu.SemaphoreType.DMA((groups, line)),
            pltpu.SemaphoreType.DMA((groups, plane - 1, line)),
            pltpu.SemaphoreType.DMA((groups, plane - 1, line)),
            pltpu.SemaphoreType.DMA((groups, chunks)),
            pltpu.SemaphoreType.DMA((groups, chunks)),
            pltpu.SemaphoreType.DMA((2,)),
        ],
        compiler_params=pltpu.CompilerParams(
            collective_id=0, has_side_effects=True, vmem_limit_bytes=48 * 2**20
        ),
        cost_estimate=pl.CostEstimate(
            flops=4 * tokens * cols * picked * BLOCK_TOKENS,
            bytes_accessed=4 * tokens * cols,
            transcendentals=tokens * (cols // HEAD_SIZE) * picked * BLOCK_TOKENS,
        ),
    )(wanted, block_picks, queries, keys, values)


def line_length(mesh):
    n = mesh.shape["ctx"]
    column = mesh.devices.reshape(n, -1)[:, 0]
    places = [getattr(device, "coords", None) for device in column]
    if places[0] is not None:
        firsts = [
            next((i for i in range(n) if places[i][axis] != places[0][axis]), 0)
            for axis in range(len(places[0]))
        ]
        if 1 < max(firsts) < n and n % max(firsts) == 0:
            return n // max(firsts)
    return next(a for a in range(math.isqrt(n), 0, -1) if n % a == 0)


def solution(mesh):
    return jax.shard_map(
        functools.partial(body, line_length(mesh)),
        mesh=mesh,
        in_specs=(P("ctx", "kvh"), P("ctx", "kvh"), P("ctx", "kvh"), P("ctx", None)),
        out_specs=P(("ctx", "kvh"), None),
        check_vma=False,
    )
```

```python
import functools
import math

import jax
import jax.numpy as jnp
from jax import lax
from jax.experimental import pallas as pl
from jax.experimental.pallas import tpu as pltpu
from jax.sharding import PartitionSpec as P

HEAD_SIZE = 128
BLOCK_TOKENS = 128
MESH = pl.DeviceIdType.MESH


def attend_kernel(n, line, parts, groups, blocks, picked, width, *refs):
    (req_ref, picks_ref, q_hbm, k_hbm, v_hbm, out_ref), rest = refs[:6], refs[6:]
    owns, rest = rest[:groups], rest[groups:]
    from_left, rest = rest[: groups * (line - 1)], rest[groups * (line - 1) :]
    from_right, rest = rest[: groups * (line - 1)], rest[groups * (line - 1) :]
    stages, rest = rest[:groups], rest[groups:]
    chosen, rest = rest[:groups], rest[groups:]
    (
        asked,
        asked_smem,
        q_ref,
        k_ref,
        v_ref,
        o_ref,
        k_sel,
        v_sel,
        ask_send,
        ask_recv,
        right_send,
        left_recv,
        left_send,
        right_recv,
        plane_send,
        plane_recv,
        out_send,
        out_recv,
        local_sem,
    ) = rest
    me = lax.axis_index("ctx")
    part = lax.axis_index("kvh")
    plane = n // line
    place, seat = me // plane, lax.rem(me, plane)
    part_rows = out_ref.shape[0]
    chunk = min(BLOCK_TOKENS, part_rows)
    part_chunks = part_rows // chunk
    block_chunks = BLOCK_TOKENS // chunk
    cols = groups * width

    k_copy = pltpu.make_async_copy(k_hbm, k_ref, local_sem.at[2])
    v_copy = pltpu.make_async_copy(v_hbm, v_ref, local_sem.at[3])
    q_copy = pltpu.make_async_copy(q_hbm, q_ref, local_sem.at[0])
    k_copy.start()
    v_copy.start()
    q_copy.start()

    barrier = pltpu.get_barrier_semaphore()

    def greet_ctx(d, _):
        peer = lax.rem(me + d, n)
        pl.semaphore_signal(barrier, inc=1, device_id=(peer, part), device_id_type=MESH)
        return 0

    def greet_kvh(d, _):
        peer = lax.rem(part + d, parts)
        pl.semaphore_signal(barrier, inc=1, device_id=(me, peer), device_id_type=MESH)
        return 0

    lax.fori_loop(1, n, greet_ctx, 0)
    lax.fori_loop(1, parts, greet_kvh, 0)

    def pack(g):
        lanes = slice(g * HEAD_SIZE, (g + 1) * HEAD_SIZE)
        for i in range(blocks):
            owns[g][i, :BLOCK_TOKENS, :] = k_ref[i, :, lanes]
            owns[g][i, BLOCK_TOKENS:, :] = v_ref[i, :, lanes]

    asked[plane - 1] = req_ref[...]
    v_sel[:, HEAD_SIZE:] = jnp.ones((picked * BLOCK_TOKENS, HEAD_SIZE), jnp.bfloat16)
    k_copy.wait()
    v_copy.wait()
    for g in range(groups):
        pack(g)
    pl.semaphore_wait(barrier, n - 1 + parts - 1)

    def over_peers(action):
        def one(d, _):
            action(d)
            return 0

        lax.fori_loop(1, plane, one, 0)

    def plane_peer(d):
        return (place * plane + lax.rem(seat + d, plane), part)

    def ask_copy(d):
        return pltpu.make_async_remote_copy(
            src_ref=req_ref,
            dst_ref=asked.at[plane - 1 - d],
            send_sem=ask_send.at[d - 1],
            recv_sem=ask_recv.at[plane - 1 - d],
            device_id=plane_peer(d),
            device_id_type=MESH,
        )

    def right_copy(g, k):
        return pltpu.make_async_remote_copy(
            src_ref=owns[g] if k == 0 else from_left[g * (line - 1) + k - 1],
            dst_ref=from_left[g * (line - 1) + k],
            send_sem=right_send.at[g, k],
            recv_sem=left_recv.at[g, k],
            device_id=(me + plane, part),
            device_id_type=MESH,
        )

    def left_copy(g, k):
        return pltpu.make_async_remote_copy(
            src_ref=owns[g] if k == 0 else from_right[g * (line - 1) + k - 1],
            dst_ref=from_right[g * (line - 1) + k],
            send_sem=left_send.at[g, k],
            recv_sem=right_recv.at[g, k],
            device_id=(me - plane, part),
            device_id_type=MESH,
        )

    def plane_copy(g, d, source):
        return pltpu.make_async_remote_copy(
            src_ref=stages[g].at[d - 1, source],
            dst_ref=chosen[g].at[plane - 1 - d, source],
            send_sem=plane_send.at[g, d - 1, source],
            recv_sem=plane_recv.at[g, plane - 1 - d, source],
            device_id=plane_peer(d),
            device_id_type=MESH,
        )

    def share(g, shard, source):
        owner = source * plane + seat

        def one(d):
            wanted = asked_smem[d - 1, 0, owner]
            stages[g][d - 1, source] = shard[wanted]
            plane_copy(g, d, source).start()

        over_peers(one)
        chosen[g][plane - 1, source] = shard[asked_smem[plane - 1, 0, owner]]

    def begin(g):
        @pl.when(place < line - 1)
        def _():
            right_copy(g, 0).start()

        @pl.when(place > 0)
        def _():
            left_copy(g, 0).start()

    def hop(g, k):
        last = line - 1

        @pl.when(place >= k)
        def _():
            right_copy(g, k - 1).wait_recv()
            if k < last:

                @pl.when(place < last)
                def _():
                    right_copy(g, k).start()

        @pl.when(place + k <= last)
        def _():
            left_copy(g, k - 1).wait_recv()
            if k < last:

                @pl.when(place > 0)
                def _():
                    left_copy(g, k).start()

        if k == 1 and g + 1 < groups:
            begin(g + 1)
            share(g + 1, owns[g + 1], place)

        @pl.when(place >= k)
        def _():
            share(g, from_left[g * (line - 1) + k - 1], place - k)

        @pl.when(place + k <= last)
        def _():
            share(g, from_right[g * (line - 1) + k - 1], place + k)

    def wait_chosen(g):
        def one(d):
            def source(i, _):
                plane_copy(g, d, i).wait_recv()
                return 0

            lax.fori_loop(0, line, source, 0)

        over_peers(one)

    over_peers(lambda d: ask_copy(d).start())
    begin(0)
    over_peers(lambda d: ask_copy(d).wait_recv())
    to_smem = pltpu.make_async_copy(asked, asked_smem, local_sem.at[1])
    to_smem.start()
    to_smem.wait()
    share(0, owns[0], place)
    for k in range(1, line):
        hop(0, k)
    q_copy.wait()

    scale = math.log2(math.e) / math.sqrt(HEAD_SIZE)
    first_block = lax.rem(part + 1, parts) * part_rows // BLOCK_TOKENS

    def out_remote(g, index):
        target = index // part_chunks
        row = pl.multiple_of(lax.rem(index, part_chunks) * chunk, chunk)
        col = pl.multiple_of(part * cols + g * width, HEAD_SIZE)
        src_row = pl.multiple_of(index * chunk, chunk)
        src_col = pl.multiple_of(g * width, HEAD_SIZE)
        src = o_ref.at[pl.ds(src_row, chunk), pl.ds(src_col, width)]
        dst = out_ref.at[pl.ds(row, chunk), pl.ds(col, width)]
        slot = part * part_chunks + lax.rem(index, part_chunks)
        remote = pltpu.make_async_remote_copy(
            src_ref=src,
            dst_ref=dst,
            send_sem=out_send.at[g, index],
            recv_sem=out_recv.at[g, slot],
            device_id=(me, target),
            device_id_type=MESH,
        )
        local = pltpu.make_async_copy(src, dst, out_send.at[g, index])
        return target, remote, local

    hop_turn = {k: (k - 1) * blocks // (line - 1) + (1 if k > 1 else 0) for k in range(1, line)}
    hop_turn = {k: min(turn, blocks - 1) for k, turn in hop_turn.items()}

    def step(t, _):
        g = t // blocks
        turn = lax.rem(t, blocks)
        b = lax.rem(first_block + turn, blocks)
        for gi in range(groups):
            for ti in range(blocks):
                hops = [k for k in range(1, line) if hop_turn[k] == ti and gi + 1 < groups]
                if not hops and ti > 0:
                    continue

                @pl.when(jnp.logical_and(g == gi, turn == ti))
                def _():
                    for k in hops:
                        hop(gi + 1, k)
                    if ti == 0:
                        wait_chosen(gi)

            @pl.when(g == gi)
            def _():
                lanes = slice(gi * HEAD_SIZE, (gi + 1) * HEAD_SIZE)
                k_sel[:BLOCK_TOKENS, :] = k_ref[b, :, lanes]
                v_sel[:BLOCK_TOKENS, :HEAD_SIZE] = v_ref[b, :, lanes]
                for j in range(1, picked):
                    owner = picks_ref[b, j] // blocks
                    slot = lax.rem(lax.rem(owner, plane) + (plane - 1) - seat + plane, plane)
                    rows = slice(j * BLOCK_TOKENS, (j + 1) * BLOCK_TOKENS)
                    k_sel[rows, :] = chosen[gi][slot, owner // plane, :BLOCK_TOKENS, :]
                    v_sel[rows, :HEAD_SIZE] = chosen[gi][slot, owner // plane, BLOCK_TOKENS:, :]

        q_rows = pl.ds(pl.multiple_of(b * BLOCK_TOKENS, BLOCK_TOKENS), BLOCK_TOKENS)
        heads = width // HEAD_SIZE
        pair = 2 if heads % 2 == 0 else 1
        row_id = lax.broadcasted_iota(jnp.int32, (pair * BLOCK_TOKENS, BLOCK_TOKENS), 0)
        key_id = lax.broadcasted_iota(jnp.int32, (pair * BLOCK_TOKENS, BLOCK_TOKENS), 1)
        causal = key_id <= lax.rem(row_id, BLOCK_TOKENS)
        span = picked * BLOCK_TOKENS
        tile = 2 * BLOCK_TOKENS if span % (2 * BLOCK_TOKENS) == 0 else BLOCK_TOKENS

        def lanes_of(h):
            start = pl.multiple_of(g * width + h * HEAD_SIZE, HEAD_SIZE)
            return pl.ds(start, HEAD_SIZE)

        def load_queries(h):
            return jnp.concatenate([q_ref[q_rows, lanes_of(h + u)] for u in range(pair)], axis=0)

        def score_tile(q, start):
            keys = k_sel[start : start + tile, :]
            scores = lax.dot_general(
                q, keys, (((1,), (1,)), ((), ())), preferred_element_type=jnp.float32
            )
            if start == 0:
                own = jnp.where(causal, scores[:, :BLOCK_TOKENS], -jnp.inf)
                scores = jnp.concatenate([own, scores[:, BLOCK_TOKENS:]], axis=1)
            return scores

        starts = range(0, span, tile)
        q = load_queries(0)
        tiles = [score_tile(q, start) for start in starts]
        for h in range(0, heads, pair):
            top = functools.reduce(jnp.maximum, tiles)
            top = jnp.max(top, axis=1, keepdims=True)
            more = h + pair < heads
            if more:
                q = load_queries(h + pair)
            weights, following = [], []
            for scores, start in zip(tiles, starts):
                if more:
                    following.append(score_tile(q, start))
                weights.append(jnp.exp2((scores - top) * scale).astype(jnp.bfloat16))
            weights = jnp.concatenate(weights, axis=1)
            both = jnp.dot(weights, v_sel[...], preferred_element_type=jnp.float32)
            result = (both[:, :HEAD_SIZE] / both[:, HEAD_SIZE:]).astype(jnp.bfloat16)
            for u in range(pair):
                o_ref[q_rows, lanes_of(h + u)] = result[u * BLOCK_TOKENS : (u + 1) * BLOCK_TOKENS]
            tiles = following
        for c in range(block_chunks):
            target, remote, local = out_remote(g, b * block_chunks + c)

            @pl.when(target != part)
            def _():
                remote.start()

            @pl.when(target == part)
            def _():
                local.start()

        return 0

    lax.fori_loop(0, groups * blocks, step, 0)

    def finish(t, _):
        g = t // (parts * part_chunks)
        index = lax.rem(t, parts * part_chunks)
        target, remote, local = out_remote(g, index)

        @pl.when(target != part)
        def _():
            remote.wait_send()
            row = pl.multiple_of(lax.rem(index, part_chunks) * chunk, chunk)
            col = pl.multiple_of(target * cols + g * width, HEAD_SIZE)
            landed = out_ref.at[pl.ds(row, chunk), pl.ds(col, width)]
            pltpu.make_async_remote_copy(
                src_ref=landed,
                dst_ref=landed,
                send_sem=out_send.at[g, index],
                recv_sem=out_recv.at[g, index],
                device_id=(me, target),
                device_id_type=MESH,
            ).wait_recv()

        @pl.when(target == part)
        def _():
            local.wait()

        return 0

    def plane_done(d):
        for g in range(groups):

            def source(i, _):
                plane_copy(g, d, i).wait_send()
                return 0

            lax.fori_loop(0, line, source, 0)

    over_peers(lambda d: ask_copy(d).wait_send())
    over_peers(plane_done)
    for g in range(groups):
        for k in range(line - 1):

            @pl.when(jnp.logical_and(place < line - 1, place >= k))
            def _():
                right_copy(g, k).wait_send()

            @pl.when(jnp.logical_and(place > 0, place + k <= line - 1))
            def _():
                left_copy(g, k).wait_send()

    lax.fori_loop(0, groups * parts * part_chunks, finish, 0)


def body(line, queries, key_vector_rows, value_vector_rows, block_picks):
    n = lax.axis_size("ctx")
    parts = lax.axis_size("kvh")
    tokens, cols = queries.shape
    blocks = tokens // BLOCK_TOKENS
    picked = block_picks.shape[1]
    groups = key_vector_rows.shape[1] // HEAD_SIZE
    width = cols // groups
    keys = key_vector_rows.reshape(blocks, BLOCK_TOKENS, groups * HEAD_SIZE)
    values = value_vector_rows.reshape(blocks, BLOCK_TOKENS, groups * HEAD_SIZE)
    remote = block_picks[:, 1:].reshape(-1)
    owned = (remote // blocks)[None, :] == jnp.arange(n, dtype=jnp.int32)[:, None]
    wanted = jnp.max(jnp.where(owned, (remote % blocks)[None, :], 0), axis=1)
    lanes = -(-n // 128) * 128
    wanted = jnp.pad(wanted, (0, lanes - n)).reshape(1, lanes)

    vmem = pl.BlockSpec(memory_space=pltpu.VMEM)
    anywhere = pl.BlockSpec(memory_space=pl.ANY)
    part_rows = tokens // parts
    chunks = tokens // min(BLOCK_TOKENS, part_rows)
    plane = n // line
    shard = pltpu.VMEM((blocks, 2 * BLOCK_TOKENS, HEAD_SIZE), jnp.bfloat16)
    stage = pltpu.VMEM((plane - 1, line, 2 * BLOCK_TOKENS, HEAD_SIZE), jnp.bfloat16)
    slots = pltpu.VMEM((plane, line, 2 * BLOCK_TOKENS, HEAD_SIZE), jnp.bfloat16)
    return pl.pallas_call(
        functools.partial(attend_kernel, n, line, parts, groups, blocks, picked, width),
        out_shape=jax.ShapeDtypeStruct((part_rows, parts * cols), jnp.bfloat16),
        in_specs=[vmem, pl.BlockSpec(memory_space=pltpu.SMEM), anywhere, anywhere, anywhere],
        out_specs=anywhere,
        scratch_shapes=[shard] * (groups * (2 * line - 1))
        + [stage] * groups
        + [slots] * groups
        + [
            pltpu.VMEM((plane, 1, lanes), jnp.int32),
            pltpu.SMEM((plane, 1, lanes), jnp.int32),
            pltpu.VMEM((tokens, cols), jnp.bfloat16),
            pltpu.VMEM(keys.shape, jnp.bfloat16),
            pltpu.VMEM(values.shape, jnp.bfloat16),
            pltpu.VMEM((tokens, cols), jnp.bfloat16),
            pltpu.VMEM((picked * BLOCK_TOKENS, HEAD_SIZE), jnp.bfloat16),
            pltpu.VMEM((picked * BLOCK_TOKENS, 2 * HEAD_SIZE), jnp.bfloat16),
            pltpu.SemaphoreType.DMA((plane - 1,)),
            pltpu.SemaphoreType.DMA((plane - 1,)),
            pltpu.SemaphoreType.DMA((groups, line)),
            pltpu.SemaphoreType.DMA((groups, line)),
            pltpu.SemaphoreType.DMA((groups, line)),
            pltpu.SemaphoreType.DMA((groups, line)),
            pltpu.SemaphoreType.DMA((groups, plane - 1, line)),
            pltpu.SemaphoreType.DMA((groups, plane - 1, line)),
            pltpu.SemaphoreType.DMA((groups, chunks)),
            pltpu.SemaphoreType.DMA((groups, chunks)),
            pltpu.SemaphoreType.DMA((4,)),
        ],
        compiler_params=pltpu.CompilerParams(
            collective_id=0, has_side_effects=True, vmem_limit_bytes=48 * 2**20
        ),
        cost_estimate=pl.CostEstimate(
            flops=4 * tokens * cols * picked * BLOCK_TOKENS,
            bytes_accessed=4 * tokens * cols,
            transcendentals=tokens * (cols // HEAD_SIZE) * picked * BLOCK_TOKENS,
        ),
    )(wanted, block_picks, queries, keys, values)


def line_length(mesh):
    n = mesh.shape["ctx"]
    column = mesh.devices.reshape(n, -1)[:, 0]
    places = [getattr(device, "coords", None) for device in column]
    if places[0] is not None:
        firsts = [
            next((i for i in range(n) if places[i][axis] != places[0][axis]), 0)
            for axis in range(len(places[0]))
        ]
        if 1 < max(firsts) < n and n % max(firsts) == 0:
            return n // max(firsts)
    return next(a for a in range(math.isqrt(n), 0, -1) if n % a == 0)


def solution(mesh):
    return jax.shard_map(
        functools.partial(body, line_length(mesh)),
        mesh=mesh,
        in_specs=(P("ctx", "kvh"), P("ctx", "kvh"), P("ctx", "kvh"), P("ctx", None)),
        out_specs=P(("ctx", "kvh"), None),
        check_vma=False,
    )
```

```python
import functools
import math

import jax
import jax.numpy as jnp
from jax import lax
from jax.experimental import pallas as pl
from jax.experimental.pallas import tpu as pltpu
from jax.sharding import PartitionSpec as P

HEAD_SIZE = 128
BLOCK_TOKENS = 128
MESH = pl.DeviceIdType.MESH


def attend_kernel(n, line, parts, groups, blocks, picked, width, *refs):
    (req_ref, picks_ref, q_hbm, k_hbm, v_hbm, out_ref), rest = refs[:6], refs[6:]
    owns, rest = rest[:groups], rest[groups:]
    from_left, rest = rest[: groups * (line - 1)], rest[groups * (line - 1) :]
    from_right, rest = rest[: groups * (line - 1)], rest[groups * (line - 1) :]
    stages, rest = rest[:groups], rest[groups:]
    chosen, rest = rest[:groups], rest[groups:]
    (
        asked,
        asked_smem,
        q_ref,
        k_ref,
        v_ref,
        o_ref,
        k_sel,
        v_sel,
        ask_send,
        ask_recv,
        right_send,
        left_recv,
        left_send,
        right_recv,
        plane_send,
        plane_recv,
        out_send,
        out_recv,
        local_sem,
    ) = rest
    me = lax.axis_index("ctx")
    part = lax.axis_index("kvh")
    plane = n // line
    place, seat = me // plane, lax.rem(me, plane)
    part_rows = out_ref.shape[0]
    chunk = min(BLOCK_TOKENS, part_rows)
    part_chunks = part_rows // chunk
    block_chunks = BLOCK_TOKENS // chunk
    cols = groups * width

    k_copy = pltpu.make_async_copy(k_hbm, k_ref, local_sem.at[2])
    v_copy = pltpu.make_async_copy(v_hbm, v_ref, local_sem.at[3])
    q_copy = pltpu.make_async_copy(q_hbm, q_ref, local_sem.at[0])
    k_copy.start()
    v_copy.start()
    q_copy.start()

    barrier = pltpu.get_barrier_semaphore()

    def greet_ctx(d, _):
        peer = lax.rem(me + d, n)
        pl.semaphore_signal(barrier, inc=1, device_id=(peer, part), device_id_type=MESH)
        return 0

    def greet_kvh(d, _):
        peer = lax.rem(part + d, parts)
        pl.semaphore_signal(barrier, inc=1, device_id=(me, peer), device_id_type=MESH)
        return 0

    lax.fori_loop(1, n, greet_ctx, 0)
    lax.fori_loop(1, parts, greet_kvh, 0)

    def pack(g):
        lanes = slice(g * HEAD_SIZE, (g + 1) * HEAD_SIZE)
        for i in range(blocks):
            keys = k_ref[i, :, lanes].astype(jnp.float32).T
            owns[g][i, :HEAD_SIZE, :] = keys.astype(jnp.bfloat16)
            owns[g][i, HEAD_SIZE:, :] = v_ref[i, :, lanes]

    asked[plane - 1] = req_ref[...]
    v_sel[:, HEAD_SIZE:] = jnp.ones((picked * BLOCK_TOKENS, HEAD_SIZE), jnp.bfloat16)
    k_copy.wait()
    v_copy.wait()
    pack(0)
    pl.semaphore_wait(barrier, n - 1 + parts - 1)

    def over_peers(action):
        def one(d, _):
            action(d)
            return 0

        lax.fori_loop(1, plane, one, 0)

    def plane_peer(d):
        return (place * plane + lax.rem(seat + d, plane), part)

    def ask_copy(d):
        return pltpu.make_async_remote_copy(
            src_ref=req_ref,
            dst_ref=asked.at[plane - 1 - d],
            send_sem=ask_send.at[d - 1],
            recv_sem=ask_recv.at[plane - 1 - d],
            device_id=plane_peer(d),
            device_id_type=MESH,
        )

    def right_copy(g, k):
        return pltpu.make_async_remote_copy(
            src_ref=owns[g] if k == 0 else from_left[g * (line - 1) + k - 1],
            dst_ref=from_left[g * (line - 1) + k],
            send_sem=right_send.at[g, k],
            recv_sem=left_recv.at[g, k],
            device_id=(me + plane, part),
            device_id_type=MESH,
        )

    def left_copy(g, k):
        return pltpu.make_async_remote_copy(
            src_ref=owns[g] if k == 0 else from_right[g * (line - 1) + k - 1],
            dst_ref=from_right[g * (line - 1) + k],
            send_sem=left_send.at[g, k],
            recv_sem=right_recv.at[g, k],
            device_id=(me - plane, part),
            device_id_type=MESH,
        )

    def plane_copy(g, d, source):
        return pltpu.make_async_remote_copy(
            src_ref=stages[g].at[d - 1, source],
            dst_ref=chosen[g].at[plane - 1 - d, source],
            send_sem=plane_send.at[g, d - 1, source],
            recv_sem=plane_recv.at[g, plane - 1 - d, source],
            device_id=plane_peer(d),
            device_id_type=MESH,
        )

    def share(g, shard, source):
        owner = source * plane + seat

        def one(d):
            wanted = asked_smem[d - 1, 0, owner]
            stages[g][d - 1, source] = shard[wanted]
            plane_copy(g, d, source).start()

        over_peers(one)
        chosen[g][plane - 1, source] = shard[asked_smem[plane - 1, 0, owner]]

    def begin(g):
        @pl.when(place < line - 1)
        def _():
            right_copy(g, 0).start()

        @pl.when(place > 0)
        def _():
            left_copy(g, 0).start()

    def hop(g, k):
        last = line - 1

        @pl.when(place >= k)
        def _():
            right_copy(g, k - 1).wait_recv()
            if k < last:

                @pl.when(place < last)
                def _():
                    right_copy(g, k).start()

        @pl.when(place + k <= last)
        def _():
            left_copy(g, k - 1).wait_recv()
            if k < last:

                @pl.when(place > 0)
                def _():
                    left_copy(g, k).start()

        if k == 1 and g + 1 < groups:
            pack(g + 1)
            begin(g + 1)
            share(g + 1, owns[g + 1], place)

        @pl.when(place >= k)
        def _():
            share(g, from_left[g * (line - 1) + k - 1], place - k)

        @pl.when(place + k <= last)
        def _():
            share(g, from_right[g * (line - 1) + k - 1], place + k)

    def wait_chosen(g):
        def one(d):
            def source(i, _):
                plane_copy(g, d, i).wait_recv()
                return 0

            lax.fori_loop(0, line, source, 0)

        over_peers(one)

    over_peers(lambda d: ask_copy(d).start())
    begin(0)
    over_peers(lambda d: ask_copy(d).wait_recv())
    to_smem = pltpu.make_async_copy(asked, asked_smem, local_sem.at[1])
    to_smem.start()
    to_smem.wait()
    share(0, owns[0], place)
    for k in range(1, line):
        hop(0, k)
    q_copy.wait()

    scale = math.log2(math.e) / math.sqrt(HEAD_SIZE)
    first_block = lax.rem(part + 1, parts) * part_rows // BLOCK_TOKENS

    def out_remote(g, index):
        target = index // part_chunks
        row = pl.multiple_of(lax.rem(index, part_chunks) * chunk, chunk)
        col = pl.multiple_of(part * cols + g * width, HEAD_SIZE)
        src_row = pl.multiple_of(index * chunk, chunk)
        src_col = pl.multiple_of(g * width, HEAD_SIZE)
        src = o_ref.at[pl.ds(src_row, chunk), pl.ds(src_col, width)]
        dst = out_ref.at[pl.ds(row, chunk), pl.ds(col, width)]
        slot = part * part_chunks + lax.rem(index, part_chunks)
        remote = pltpu.make_async_remote_copy(
            src_ref=src,
            dst_ref=dst,
            send_sem=out_send.at[g, index],
            recv_sem=out_recv.at[g, slot],
            device_id=(me, target),
            device_id_type=MESH,
        )
        local = pltpu.make_async_copy(src, dst, out_send.at[g, index])
        return target, remote, local

    hop_turn = {k: (k - 1) * blocks // (line - 1) + (1 if k > 1 else 0) for k in range(1, line)}
    hop_turn = {k: min(turn, blocks - 1) for k, turn in hop_turn.items()}

    def step(t, _):
        g = t // blocks
        turn = lax.rem(t, blocks)
        b = lax.rem(first_block + turn, blocks)
        for gi in range(groups):
            for ti in range(blocks):
                hops = [k for k in range(1, line) if hop_turn[k] == ti and gi + 1 < groups]
                if not hops and ti > 0:
                    continue

                @pl.when(jnp.logical_and(g == gi, turn == ti))
                def _():
                    for k in hops:
                        hop(gi + 1, k)
                    if ti == 0:
                        wait_chosen(gi)

            @pl.when(g == gi)
            def _():
                k_sel[:, :BLOCK_TOKENS] = owns[gi][b, :HEAD_SIZE, :]
                v_sel[:BLOCK_TOKENS, :HEAD_SIZE] = owns[gi][b, HEAD_SIZE:, :]
                for j in range(1, picked):
                    owner = picks_ref[b, j] // blocks
                    slot = lax.rem(lax.rem(owner, plane) + (plane - 1) - seat + plane, plane)
                    rows = slice(j * BLOCK_TOKENS, (j + 1) * BLOCK_TOKENS)
                    k_sel[:, rows] = chosen[gi][slot, owner // plane, :HEAD_SIZE, :]
                    v_sel[rows, :HEAD_SIZE] = chosen[gi][slot, owner // plane, HEAD_SIZE:, :]

        q_rows = pl.ds(pl.multiple_of(b * BLOCK_TOKENS, BLOCK_TOKENS), BLOCK_TOKENS)
        heads = width // HEAD_SIZE
        pair = 2 if heads % 2 == 0 else 1
        row_id = lax.broadcasted_iota(jnp.int32, (pair * BLOCK_TOKENS, BLOCK_TOKENS), 0)
        key_id = lax.broadcasted_iota(jnp.int32, (pair * BLOCK_TOKENS, BLOCK_TOKENS), 1)
        causal = key_id <= lax.rem(row_id, BLOCK_TOKENS)
        span = picked * BLOCK_TOKENS
        tile = 2 * BLOCK_TOKENS if span % (2 * BLOCK_TOKENS) == 0 else BLOCK_TOKENS

        def lanes_of(h):
            start = pl.multiple_of(g * width + h * HEAD_SIZE, HEAD_SIZE)
            return pl.ds(start, HEAD_SIZE)

        def load_queries(h):
            return jnp.concatenate([q_ref[q_rows, lanes_of(h + u)] for u in range(pair)], axis=0)

        def score_tile(q, start):
            keys = k_sel[:, start : start + tile]
            scores = jnp.dot(q, keys, preferred_element_type=jnp.float32)
            if start == 0:
                own = jnp.where(causal, scores[:, :BLOCK_TOKENS], -jnp.inf)
                scores = jnp.concatenate([own, scores[:, BLOCK_TOKENS:]], axis=1)
            return scores

        starts = range(0, span, tile)
        q = load_queries(0)
        tiles = [score_tile(q, start) for start in starts]
        for h in range(0, heads, pair):
            top = functools.reduce(jnp.maximum, tiles)
            top = jnp.max(top, axis=1, keepdims=True)
            more = h + pair < heads
            if more:
                q = load_queries(h + pair)
            weights, following = [], []
            for scores, start in zip(tiles, starts):
                if more:
                    following.append(score_tile(q, start))
                weights.append(jnp.exp2((scores - top) * scale).astype(jnp.bfloat16))
            weights = jnp.concatenate(weights, axis=1)
            both = jnp.dot(weights, v_sel[...], preferred_element_type=jnp.float32)
            result = (both[:, :HEAD_SIZE] / both[:, HEAD_SIZE:]).astype(jnp.bfloat16)
            for u in range(pair):
                o_ref[q_rows, lanes_of(h + u)] = result[u * BLOCK_TOKENS : (u + 1) * BLOCK_TOKENS]
            tiles = following
        for c in range(block_chunks):
            target, remote, local = out_remote(g, b * block_chunks + c)

            @pl.when(target != part)
            def _():
                remote.start()

            @pl.when(target == part)
            def _():
                local.start()

        return 0

    lax.fori_loop(0, groups * blocks, step, 0)

    def finish(t, _):
        g = t // (parts * part_chunks)
        index = lax.rem(t, parts * part_chunks)
        target, remote, local = out_remote(g, index)

        @pl.when(target != part)
        def _():
            remote.wait_send()
            row = pl.multiple_of(lax.rem(index, part_chunks) * chunk, chunk)
            col = pl.multiple_of(target * cols + g * width, HEAD_SIZE)
            landed = out_ref.at[pl.ds(row, chunk), pl.ds(col, width)]
            pltpu.make_async_remote_copy(
                src_ref=landed,
                dst_ref=landed,
                send_sem=out_send.at[g, index],
                recv_sem=out_recv.at[g, index],
                device_id=(me, target),
                device_id_type=MESH,
            ).wait_recv()

        @pl.when(target == part)
        def _():
            local.wait()

        return 0

    def plane_done(d):
        for g in range(groups):

            def source(i, _):
                plane_copy(g, d, i).wait_send()
                return 0

            lax.fori_loop(0, line, source, 0)

    over_peers(lambda d: ask_copy(d).wait_send())
    over_peers(plane_done)
    for g in range(groups):
        for k in range(line - 1):

            @pl.when(jnp.logical_and(place < line - 1, place >= k))
            def _():
                right_copy(g, k).wait_send()

            @pl.when(jnp.logical_and(place > 0, place + k <= line - 1))
            def _():
                left_copy(g, k).wait_send()

    lax.fori_loop(0, groups * parts * part_chunks, finish, 0)


def body(line, queries, key_vector_rows, value_vector_rows, block_picks):
    n = lax.axis_size("ctx")
    parts = lax.axis_size("kvh")
    tokens, cols = queries.shape
    blocks = tokens // BLOCK_TOKENS
    picked = block_picks.shape[1]
    groups = key_vector_rows.shape[1] // HEAD_SIZE
    width = cols // groups
    keys = key_vector_rows.reshape(blocks, BLOCK_TOKENS, groups * HEAD_SIZE)
    values = value_vector_rows.reshape(blocks, BLOCK_TOKENS, groups * HEAD_SIZE)
    owned = (block_picks // blocks)[None] == jnp.arange(n, dtype=jnp.int32)[:, None, None]
    wanted = jnp.max(jnp.where(owned, (block_picks % blocks)[None], 0), axis=(1, 2))
    lanes = -(-n // 128) * 128
    wanted = jnp.pad(wanted, (0, lanes - n)).reshape(1, lanes)

    vmem = pl.BlockSpec(memory_space=pltpu.VMEM)
    anywhere = pl.BlockSpec(memory_space=pl.ANY)
    part_rows = tokens // parts
    chunks = tokens // min(BLOCK_TOKENS, part_rows)
    plane = n // line
    shard = pltpu.VMEM((blocks, 2 * BLOCK_TOKENS, HEAD_SIZE), jnp.bfloat16)
    stage = pltpu.VMEM((plane - 1, line, 2 * BLOCK_TOKENS, HEAD_SIZE), jnp.bfloat16)
    slots = pltpu.VMEM((plane, line, 2 * BLOCK_TOKENS, HEAD_SIZE), jnp.bfloat16)
    return pl.pallas_call(
        functools.partial(attend_kernel, n, line, parts, groups, blocks, picked, width),
        out_shape=jax.ShapeDtypeStruct((part_rows, parts * cols), jnp.bfloat16),
        in_specs=[vmem, pl.BlockSpec(memory_space=pltpu.SMEM), anywhere, anywhere, anywhere],
        out_specs=anywhere,
        scratch_shapes=[shard] * (groups * (2 * line - 1))
        + [stage] * groups
        + [slots] * groups
        + [
            pltpu.VMEM((plane, 1, lanes), jnp.int32),
            pltpu.SMEM((plane, 1, lanes), jnp.int32),
            pltpu.VMEM((tokens, cols), jnp.bfloat16),
            pltpu.VMEM(keys.shape, jnp.bfloat16),
            pltpu.VMEM(values.shape, jnp.bfloat16),
            pltpu.VMEM((tokens, cols), jnp.bfloat16),
            pltpu.VMEM((HEAD_SIZE, picked * BLOCK_TOKENS), jnp.bfloat16),
            pltpu.VMEM((picked * BLOCK_TOKENS, 2 * HEAD_SIZE), jnp.bfloat16),
            pltpu.SemaphoreType.DMA((plane - 1,)),
            pltpu.SemaphoreType.DMA((plane - 1,)),
            pltpu.SemaphoreType.DMA((groups, line)),
            pltpu.SemaphoreType.DMA((groups, line)),
            pltpu.SemaphoreType.DMA((groups, line)),
            pltpu.SemaphoreType.DMA((groups, line)),
            pltpu.SemaphoreType.DMA((groups, plane - 1, line)),
            pltpu.SemaphoreType.DMA((groups, plane - 1, line)),
            pltpu.SemaphoreType.DMA((groups, chunks)),
            pltpu.SemaphoreType.DMA((groups, chunks)),
            pltpu.SemaphoreType.DMA((4,)),
        ],
        compiler_params=pltpu.CompilerParams(
            collective_id=0, has_side_effects=True, vmem_limit_bytes=60 * 2**20
        ),
        cost_estimate=pl.CostEstimate(
            flops=4 * tokens * cols * picked * BLOCK_TOKENS,
            bytes_accessed=4 * tokens * cols,
            transcendentals=tokens * (cols // HEAD_SIZE) * picked * BLOCK_TOKENS,
        ),
    )(wanted, block_picks, queries, keys, values)


def line_length(mesh):
    n = mesh.shape["ctx"]
    column = mesh.devices.reshape(n, -1)[:, 0]
    places = [getattr(device, "coords", None) for device in column]
    if places[0] is not None:
        firsts = [
            next((i for i in range(n) if places[i][axis] != places[0][axis]), 0)
            for axis in range(len(places[0]))
        ]
        if 1 < max(firsts) < n and n % max(firsts) == 0:
            return n // max(firsts)
    return next(a for a in range(math.isqrt(n), 0, -1) if n % a == 0)


def solution(mesh):
    return jax.shard_map(
        functools.partial(body, line_length(mesh)),
        mesh=mesh,
        in_specs=(P("ctx", "kvh"), P("ctx", "kvh"), P("ctx", "kvh"), P("ctx", None)),
        out_specs=P(("ctx", "kvh"), None),
        check_vma=False,
    )
```

```python
import functools
import math

import jax
import jax.numpy as jnp
from jax import lax
from jax.experimental import pallas as pl
from jax.experimental.pallas import tpu as pltpu
from jax.sharding import PartitionSpec as P

HEAD_SIZE = 128
BLOCK_TOKENS = 128
MESH = pl.DeviceIdType.MESH


def attend_kernel(n, line, parts, groups, blocks, picked, width, *refs):
    (req_ref, picks_ref, q_hbm, k_hbm, v_hbm, out_ref), rest = refs[:6], refs[6:]
    owns, rest = rest[:groups], rest[groups:]
    from_left, rest = rest[: groups * (line - 1)], rest[groups * (line - 1) :]
    from_right, rest = rest[: groups * (line - 1)], rest[groups * (line - 1) :]
    stages, rest = rest[:groups], rest[groups:]
    chosen, rest = rest[:groups], rest[groups:]
    (
        asked,
        asked_smem,
        q_ref,
        k_ref,
        v_ref,
        o_ref,
        k_sel,
        v_sel,
        ask_send,
        ask_recv,
        right_send,
        left_recv,
        left_send,
        right_recv,
        plane_send,
        plane_recv,
        out_send,
        out_recv,
        local_sem,
    ) = rest
    me = lax.axis_index("ctx")
    part = lax.axis_index("kvh")
    plane = n // line
    place, seat = me // plane, lax.rem(me, plane)
    part_rows = out_ref.shape[0]
    chunk = min(BLOCK_TOKENS, part_rows)
    part_chunks = part_rows // chunk
    block_chunks = BLOCK_TOKENS // chunk
    cols = groups * width
    heads = width // HEAD_SIZE
    pair = 2 if heads % 2 == 0 else 1
    pieces = 2 if heads // pair % 2 == 0 else 1
    piece_cols = width // pieces

    k_copy = pltpu.make_async_copy(k_hbm, k_ref, local_sem.at[2])
    v_copy = pltpu.make_async_copy(v_hbm, v_ref, local_sem.at[3])
    q_copy = pltpu.make_async_copy(q_hbm, q_ref, local_sem.at[0])
    k_copy.start()
    v_copy.start()
    q_copy.start()

    barrier = pltpu.get_barrier_semaphore()

    def greet_ctx(d, _):
        peer = lax.rem(me + d, n)
        pl.semaphore_signal(barrier, inc=1, device_id=(peer, part), device_id_type=MESH)
        return 0

    def greet_kvh(d, _):
        peer = lax.rem(part + d, parts)
        pl.semaphore_signal(barrier, inc=1, device_id=(me, peer), device_id_type=MESH)
        return 0

    lax.fori_loop(1, n, greet_ctx, 0)
    lax.fori_loop(1, parts, greet_kvh, 0)

    def pack(g):
        lanes = slice(g * HEAD_SIZE, (g + 1) * HEAD_SIZE)
        for i in range(blocks):
            keys = k_ref[i, :, lanes].astype(jnp.float32).T
            owns[g][i, :HEAD_SIZE, :] = keys.astype(jnp.bfloat16)
            owns[g][i, HEAD_SIZE:, :] = v_ref[i, :, lanes]

    asked[plane - 1] = req_ref[...]
    v_sel[:, HEAD_SIZE:] = jnp.ones((picked * BLOCK_TOKENS, HEAD_SIZE), jnp.bfloat16)
    k_copy.wait()
    v_copy.wait()
    pack(0)
    pl.semaphore_wait(barrier, n - 1 + parts - 1)

    def over_peers(action):
        def one(d, _):
            action(d)
            return 0

        lax.fori_loop(1, plane, one, 0)

    def plane_peer(d):
        return (place * plane + lax.rem(seat + d, plane), part)

    def ask_copy(d):
        return pltpu.make_async_remote_copy(
            src_ref=req_ref,
            dst_ref=asked.at[plane - 1 - d],
            send_sem=ask_send.at[d - 1],
            recv_sem=ask_recv.at[plane - 1 - d],
            device_id=plane_peer(d),
            device_id_type=MESH,
        )

    def right_copy(g, k):
        return pltpu.make_async_remote_copy(
            src_ref=owns[g] if k == 0 else from_left[g * (line - 1) + k - 1],
            dst_ref=from_left[g * (line - 1) + k],
            send_sem=right_send.at[g, k],
            recv_sem=left_recv.at[g, k],
            device_id=(me + plane, part),
            device_id_type=MESH,
        )

    def left_copy(g, k):
        return pltpu.make_async_remote_copy(
            src_ref=owns[g] if k == 0 else from_right[g * (line - 1) + k - 1],
            dst_ref=from_right[g * (line - 1) + k],
            send_sem=left_send.at[g, k],
            recv_sem=right_recv.at[g, k],
            device_id=(me - plane, part),
            device_id_type=MESH,
        )

    def plane_copy(g, d, source):
        return pltpu.make_async_remote_copy(
            src_ref=stages[g].at[d - 1, source],
            dst_ref=chosen[g].at[plane - 1 - d, source],
            send_sem=plane_send.at[g, d - 1, source],
            recv_sem=plane_recv.at[g, plane - 1 - d, source],
            device_id=plane_peer(d),
            device_id_type=MESH,
        )

    def share(g, shard, source):
        owner = source * plane + seat

        def one(d):
            wanted = asked_smem[d - 1, 0, owner]
            stages[g][d - 1, source] = shard[wanted]
            plane_copy(g, d, source).start()

        over_peers(one)
        chosen[g][plane - 1, source] = shard[asked_smem[plane - 1, 0, owner]]

    def begin(g):
        @pl.when(place < line - 1)
        def _():
            right_copy(g, 0).start()

        @pl.when(place > 0)
        def _():
            left_copy(g, 0).start()

    def hop(g, k):
        last = line - 1

        @pl.when(place >= k)
        def _():
            right_copy(g, k - 1).wait_recv()
            if k < last:

                @pl.when(place < last)
                def _():
                    right_copy(g, k).start()

        @pl.when(place + k <= last)
        def _():
            left_copy(g, k - 1).wait_recv()
            if k < last:

                @pl.when(place > 0)
                def _():
                    left_copy(g, k).start()

        if k == 1 and g <= 1 and g + 1 < groups:
            pack(g + 1)
            begin(g + 1)
        if k == min(2, last) and g >= 1 and g + 2 < groups:
            pack(g + 2)
            begin(g + 2)
        if k == 1 and g + 1 < groups:
            share(g + 1, owns[g + 1], place)

        @pl.when(place >= k)
        def _():
            share(g, from_left[g * (line - 1) + k - 1], place - k)

        @pl.when(place + k <= last)
        def _():
            share(g, from_right[g * (line - 1) + k - 1], place + k)

    def wait_chosen(g):
        def one(d):
            def source(i, _):
                plane_copy(g, d, i).wait_recv()
                return 0

            lax.fori_loop(0, line, source, 0)

        over_peers(one)

    over_peers(lambda d: ask_copy(d).start())
    begin(0)
    over_peers(lambda d: ask_copy(d).wait_recv())
    to_smem = pltpu.make_async_copy(asked, asked_smem, local_sem.at[1])
    to_smem.start()
    to_smem.wait()
    share(0, owns[0], place)
    for k in range(1, line):
        hop(0, k)
    q_copy.wait()

    scale = math.log2(math.e) / math.sqrt(HEAD_SIZE)
    first_block = lax.rem(part + 1, parts) * part_rows // BLOCK_TOKENS

    def out_remote(g, index, piece):
        target = index // part_chunks
        row = pl.multiple_of(lax.rem(index, part_chunks) * chunk, chunk)
        col = pl.multiple_of(part * cols + g * width + piece * piece_cols, HEAD_SIZE)
        src_row = pl.multiple_of(index * chunk, chunk)
        src_col = pl.multiple_of(g * width + piece * piece_cols, HEAD_SIZE)
        src = o_ref.at[pl.ds(src_row, chunk), pl.ds(src_col, piece_cols)]
        dst = out_ref.at[pl.ds(row, chunk), pl.ds(col, piece_cols)]
        slot = part * part_chunks + lax.rem(index, part_chunks)
        remote = pltpu.make_async_remote_copy(
            src_ref=src,
            dst_ref=dst,
            send_sem=out_send.at[g, index, piece],
            recv_sem=out_recv.at[g, slot, piece],
            device_id=(me, target),
            device_id_type=MESH,
        )
        local = pltpu.make_async_copy(src, dst, out_send.at[g, index, piece])
        return target, remote, local

    hop_turn = {k: (k - 1) * blocks // (line - 1) + (1 if k > 1 else 0) for k in range(1, line)}
    hop_turn = {k: min(turn, blocks - 1) for k, turn in hop_turn.items()}

    def step(t, _):
        g = t // blocks
        turn = lax.rem(t, blocks)
        b = lax.rem(first_block + turn, blocks)
        for gi in range(groups):
            for ti in range(blocks):
                hops = [k for k in range(1, line) if hop_turn[k] == ti and gi + 1 < groups]
                if not hops and ti > 0:
                    continue

                @pl.when(jnp.logical_and(g == gi, turn == ti))
                def _():
                    for k in hops:
                        hop(gi + 1, k)
                    if ti == 0:
                        wait_chosen(gi)

            @pl.when(g == gi)
            def _():
                k_sel[:, :BLOCK_TOKENS] = owns[gi][b, :HEAD_SIZE, :]
                v_sel[:BLOCK_TOKENS, :HEAD_SIZE] = owns[gi][b, HEAD_SIZE:, :]
                for j in range(1, picked):
                    owner = picks_ref[b, j] // blocks
                    slot = lax.rem(lax.rem(owner, plane) + (plane - 1) - seat + plane, plane)
                    rows = slice(j * BLOCK_TOKENS, (j + 1) * BLOCK_TOKENS)
                    k_sel[:, rows] = chosen[gi][slot, owner // plane, :HEAD_SIZE, :]
                    v_sel[rows, :HEAD_SIZE] = chosen[gi][slot, owner // plane, HEAD_SIZE:, :]

        q_rows = pl.ds(pl.multiple_of(b * BLOCK_TOKENS, BLOCK_TOKENS), BLOCK_TOKENS)
        row_id = lax.broadcasted_iota(jnp.int32, (pair * BLOCK_TOKENS, BLOCK_TOKENS), 0)
        key_id = lax.broadcasted_iota(jnp.int32, (pair * BLOCK_TOKENS, BLOCK_TOKENS), 1)
        causal = key_id <= lax.rem(row_id, BLOCK_TOKENS)
        span = picked * BLOCK_TOKENS
        tile = 2 * BLOCK_TOKENS if span % (2 * BLOCK_TOKENS) == 0 else BLOCK_TOKENS

        def lanes_of(h):
            start = pl.multiple_of(g * width + h * HEAD_SIZE, HEAD_SIZE)
            return pl.ds(start, HEAD_SIZE)

        def load_queries(h):
            return jnp.concatenate([q_ref[q_rows, lanes_of(h + u)] for u in range(pair)], axis=0)

        def score_tile(q, start):
            keys = k_sel[:, start : start + tile]
            scores = jnp.dot(q, keys, preferred_element_type=jnp.float32)
            if start == 0:
                own = jnp.where(causal, scores[:, :BLOCK_TOKENS], -jnp.inf)
                scores = jnp.concatenate([own, scores[:, BLOCK_TOKENS:]], axis=1)
            return scores

        def send_out(piece):
            for c in range(block_chunks):
                target, remote, local = out_remote(g, b * block_chunks + c, piece)

                @pl.when(target != part)
                def _():
                    remote.start()

                @pl.when(target == part)
                def _():
                    local.start()

        starts = range(0, span, tile)
        q = load_queries(0)
        tiles = [score_tile(q, start) for start in starts]
        for h in range(0, heads, pair):
            top = functools.reduce(jnp.maximum, tiles)
            top = jnp.max(top, axis=1, keepdims=True)
            more = h + pair < heads
            if more:
                q = load_queries(h + pair)
            weights, following = [], []
            for scores, start in zip(tiles, starts):
                if more:
                    following.append(score_tile(q, start))
                weights.append(jnp.exp2((scores - top) * scale).astype(jnp.bfloat16))
            weights = jnp.concatenate(weights, axis=1)
            both = jnp.dot(weights, v_sel[...], preferred_element_type=jnp.float32)
            result = (both[:, :HEAD_SIZE] / both[:, HEAD_SIZE:]).astype(jnp.bfloat16)
            for u in range(pair):
                o_ref[q_rows, lanes_of(h + u)] = result[u * BLOCK_TOKENS : (u + 1) * BLOCK_TOKENS]
            tiles = following
            done = (h + pair) * HEAD_SIZE
            if done % piece_cols == 0:
                send_out(done // piece_cols - 1)
        return 0

    lax.fori_loop(0, groups * blocks, step, 0)

    def finish(t, _):
        g = t // (parts * part_chunks * pieces)
        index = lax.rem(t // pieces, parts * part_chunks)
        piece = lax.rem(t, pieces)
        target, remote, local = out_remote(g, index, piece)

        @pl.when(target != part)
        def _():
            remote.wait_send()
            row = pl.multiple_of(lax.rem(index, part_chunks) * chunk, chunk)
            col = pl.multiple_of(target * cols + g * width + piece * piece_cols, HEAD_SIZE)
            landed = out_ref.at[pl.ds(row, chunk), pl.ds(col, piece_cols)]
            pltpu.make_async_remote_copy(
                src_ref=landed,
                dst_ref=landed,
                send_sem=out_send.at[g, index, piece],
                recv_sem=out_recv.at[g, index, piece],
                device_id=(me, target),
                device_id_type=MESH,
            ).wait_recv()

        @pl.when(target == part)
        def _():
            local.wait()

        return 0

    def plane_done(d):
        for g in range(groups):

            def source(i, _):
                plane_copy(g, d, i).wait_send()
                return 0

            lax.fori_loop(0, line, source, 0)

    over_peers(lambda d: ask_copy(d).wait_send())
    over_peers(plane_done)
    for g in range(groups):
        for k in range(line - 1):

            @pl.when(jnp.logical_and(place < line - 1, place >= k))
            def _():
                right_copy(g, k).wait_send()

            @pl.when(jnp.logical_and(place > 0, place + k <= line - 1))
            def _():
                left_copy(g, k).wait_send()

    lax.fori_loop(0, groups * parts * part_chunks * pieces, finish, 0)


def body(line, queries, key_vector_rows, value_vector_rows, block_picks):
    n = lax.axis_size("ctx")
    parts = lax.axis_size("kvh")
    tokens, cols = queries.shape
    blocks = tokens // BLOCK_TOKENS
    picked = block_picks.shape[1]
    groups = key_vector_rows.shape[1] // HEAD_SIZE
    width = cols // groups
    keys = key_vector_rows.reshape(blocks, BLOCK_TOKENS, groups * HEAD_SIZE)
    values = value_vector_rows.reshape(blocks, BLOCK_TOKENS, groups * HEAD_SIZE)
    owned = (block_picks // blocks)[None] == jnp.arange(n, dtype=jnp.int32)[:, None, None]
    wanted = jnp.max(jnp.where(owned, (block_picks % blocks)[None], 0), axis=(1, 2))
    lanes = -(-n // 128) * 128
    wanted = jnp.pad(wanted, (0, lanes - n)).reshape(1, lanes)

    vmem = pl.BlockSpec(memory_space=pltpu.VMEM)
    anywhere = pl.BlockSpec(memory_space=pl.ANY)
    hbm = pl.BlockSpec(memory_space=pltpu.HBM)
    part_rows = tokens // parts
    chunks = tokens // min(BLOCK_TOKENS, part_rows)
    plane = n // line
    shard = pltpu.VMEM((blocks, 2 * BLOCK_TOKENS, HEAD_SIZE), jnp.bfloat16)
    stage = pltpu.VMEM((plane - 1, line, 2 * BLOCK_TOKENS, HEAD_SIZE), jnp.bfloat16)
    slots = pltpu.VMEM((plane, line, 2 * BLOCK_TOKENS, HEAD_SIZE), jnp.bfloat16)
    return pl.pallas_call(
        functools.partial(attend_kernel, n, line, parts, groups, blocks, picked, width),
        out_shape=jax.ShapeDtypeStruct((part_rows, parts * cols), jnp.bfloat16),
        in_specs=[vmem, pl.BlockSpec(memory_space=pltpu.SMEM), hbm, hbm, hbm],
        out_specs=anywhere,
        scratch_shapes=[shard] * (groups * (2 * line - 1))
        + [stage] * groups
        + [slots] * groups
        + [
            pltpu.VMEM((plane, 1, lanes), jnp.int32),
            pltpu.SMEM((plane, 1, lanes), jnp.int32),
            pltpu.VMEM((tokens, cols), jnp.bfloat16),
            pltpu.VMEM(keys.shape, jnp.bfloat16),
            pltpu.VMEM(values.shape, jnp.bfloat16),
            pltpu.VMEM((tokens, cols), jnp.bfloat16),
            pltpu.VMEM((HEAD_SIZE, picked * BLOCK_TOKENS), jnp.bfloat16),
            pltpu.VMEM((picked * BLOCK_TOKENS, 2 * HEAD_SIZE), jnp.bfloat16),
            pltpu.SemaphoreType.DMA((plane - 1,)),
            pltpu.SemaphoreType.DMA((plane - 1,)),
            pltpu.SemaphoreType.DMA((groups, line)),
            pltpu.SemaphoreType.DMA((groups, line)),
            pltpu.SemaphoreType.DMA((groups, line)),
            pltpu.SemaphoreType.DMA((groups, line)),
            pltpu.SemaphoreType.DMA((groups, plane - 1, line)),
            pltpu.SemaphoreType.DMA((groups, plane - 1, line)),
            pltpu.SemaphoreType.DMA((groups, chunks, 2)),
            pltpu.SemaphoreType.DMA((groups, chunks, 2)),
            pltpu.SemaphoreType.DMA((4,)),
        ],
        compiler_params=pltpu.CompilerParams(
            collective_id=0, has_side_effects=True, vmem_limit_bytes=48 * 2**20
        ),
        cost_estimate=pl.CostEstimate(
            flops=4 * tokens * cols * picked * BLOCK_TOKENS,
            bytes_accessed=4 * tokens * cols,
            transcendentals=tokens * (cols // HEAD_SIZE) * picked * BLOCK_TOKENS,
        ),
    )(wanted, block_picks, queries, keys, values)


def line_length(mesh):
    n = mesh.shape["ctx"]
    column = mesh.devices.reshape(n, -1)[:, 0]
    places = [getattr(device, "coords", None) for device in column]
    if places[0] is not None:
        firsts = [
            next((i for i in range(n) if places[i][axis] != places[0][axis]), 0)
            for axis in range(len(places[0]))
        ]
        if 1 < max(firsts) < n and n % max(firsts) == 0:
            return n // max(firsts)
    return next(a for a in range(math.isqrt(n), 0, -1) if n % a == 0)


def solution(mesh):
    return jax.shard_map(
        functools.partial(body, line_length(mesh)),
        mesh=mesh,
        in_specs=(P("ctx", "kvh"), P("ctx", "kvh"), P("ctx", "kvh"), P("ctx", None)),
        out_specs=P(("ctx", "kvh"), None),
        check_vma=False,
    )
```

```python
import functools
import math

import jax
import jax.numpy as jnp
from jax import lax
from jax.experimental import pallas as pl
from jax.experimental.pallas import tpu as pltpu
from jax.sharding import PartitionSpec as P

HEAD_SIZE = 128
BLOCK_TOKENS = 128
MESH = pl.DeviceIdType.MESH


def attend_kernel(n, line, parts, groups, blocks, picked, width, *refs):
    (req_ref, picks_ref, q_hbm, k_hbm, v_hbm, out_ref), rest = refs[:6], refs[6:]
    owns, rest = rest[:groups], rest[groups:]
    from_left, rest = rest[: groups * (line - 1)], rest[groups * (line - 1) :]
    from_right, rest = rest[: groups * (line - 1)], rest[groups * (line - 1) :]
    stages, rest = rest[:groups], rest[groups:]
    chosen, rest = rest[:groups], rest[groups:]
    (
        asked,
        asked_smem,
        q_ref,
        k_ref,
        v_ref,
        o_ref,
        k_sel,
        v_sel,
        ask_send,
        ask_recv,
        right_send,
        left_recv,
        left_send,
        right_recv,
        plane_send,
        plane_recv,
        out_send,
        out_recv,
        local_sem,
    ) = rest
    me = lax.axis_index("ctx")
    part = lax.axis_index("kvh")
    plane = n // line
    place, seat = me // plane, lax.rem(me, plane)
    part_rows = out_ref.shape[0]
    chunk = min(BLOCK_TOKENS, part_rows)
    part_chunks = part_rows // chunk
    block_chunks = BLOCK_TOKENS // chunk
    cols = groups * width
    heads = width // HEAD_SIZE
    pair = 2 if heads % 2 == 0 else 1
    pieces = 2 if heads // pair % 2 == 0 else 1
    piece_cols = width // pieces

    k_copy = pltpu.make_async_copy(k_hbm, k_ref, local_sem.at[2])
    v_copy = pltpu.make_async_copy(v_hbm, v_ref, local_sem.at[3])
    q_copy = pltpu.make_async_copy(q_hbm, q_ref, local_sem.at[0])
    k_copy.start()
    v_copy.start()
    q_copy.start()

    barrier = pltpu.get_barrier_semaphore()

    def greet_ctx(d, _):
        peer = lax.rem(me + d, n)
        pl.semaphore_signal(barrier, inc=1, device_id=(peer, part), device_id_type=MESH)
        return 0

    def greet_kvh(d, _):
        peer = lax.rem(part + d, parts)
        pl.semaphore_signal(barrier, inc=1, device_id=(me, peer), device_id_type=MESH)
        return 0

    lax.fori_loop(1, n, greet_ctx, 0)
    lax.fori_loop(1, parts, greet_kvh, 0)

    def pack(g):
        lanes = slice(g * HEAD_SIZE, (g + 1) * HEAD_SIZE)
        for i in range(blocks):
            keys = k_ref[i, :, lanes].astype(jnp.float32).T
            owns[g][i, :HEAD_SIZE, :] = keys.astype(jnp.bfloat16)
            owns[g][i, HEAD_SIZE:, :] = v_ref[i, :, lanes]

    asked[plane - 1] = req_ref[...]
    v_sel[:, HEAD_SIZE:] = jnp.ones((picked * BLOCK_TOKENS, HEAD_SIZE), jnp.bfloat16)
    k_copy.wait()
    v_copy.wait()
    pack(0)
    pl.semaphore_wait(barrier, n - 1 + parts - 1)

    def over_peers(action):
        def one(d, _):
            action(d)
            return 0

        lax.fori_loop(1, plane, one, 0)

    def plane_peer(d):
        return (place * plane + lax.rem(seat + d, plane), part)

    def ask_copy(d):
        return pltpu.make_async_remote_copy(
            src_ref=req_ref,
            dst_ref=asked.at[plane - 1 - d],
            send_sem=ask_send.at[d - 1],
            recv_sem=ask_recv.at[plane - 1 - d],
            device_id=plane_peer(d),
            device_id_type=MESH,
        )

    def right_copy(g, k, i):
        return pltpu.make_async_remote_copy(
            src_ref=(owns[g] if k == 0 else from_left[g * (line - 1) + k - 1]).at[i],
            dst_ref=from_left[g * (line - 1) + k].at[i],
            send_sem=right_send.at[g, k, i],
            recv_sem=left_recv.at[g, k, i],
            device_id=(me + plane, part),
            device_id_type=MESH,
        )

    def left_copy(g, k, i):
        return pltpu.make_async_remote_copy(
            src_ref=(owns[g] if k == 0 else from_right[g * (line - 1) + k - 1]).at[i],
            dst_ref=from_right[g * (line - 1) + k].at[i],
            send_sem=left_send.at[g, k, i],
            recv_sem=right_recv.at[g, k, i],
            device_id=(me - plane, part),
            device_id_type=MESH,
        )

    def plane_copy(g, d, source):
        return pltpu.make_async_remote_copy(
            src_ref=stages[g].at[d - 1, source],
            dst_ref=chosen[g].at[plane - 1 - d, source],
            send_sem=plane_send.at[g, d - 1, source],
            recv_sem=plane_recv.at[g, plane - 1 - d, source],
            device_id=plane_peer(d),
            device_id_type=MESH,
        )

    def share(g, shard, source):
        owner = source * plane + seat

        def one(d):
            wanted = asked_smem[d - 1, 0, owner]
            stages[g][d - 1, source] = shard[wanted]
            plane_copy(g, d, source).start()

        over_peers(one)
        chosen[g][plane - 1, source] = shard[asked_smem[plane - 1, 0, owner]]

    def begin(g):
        @pl.when(place < line - 1)
        def _():
            for i in range(blocks):
                right_copy(g, 0, i).start()

        @pl.when(place > 0)
        def _():
            for i in range(blocks):
                left_copy(g, 0, i).start()

    def hop(g, k):
        last = line - 1

        @pl.when(place >= k)
        def _():
            for i in range(blocks):
                right_copy(g, k - 1, i).wait_recv()
                if k < last:

                    @pl.when(place < last)
                    def _():
                        right_copy(g, k, i).start()

        @pl.when(place + k <= last)
        def _():
            for i in range(blocks):
                left_copy(g, k - 1, i).wait_recv()
                if k < last:

                    @pl.when(place > 0)
                    def _():
                        left_copy(g, k, i).start()

        if k == 1 and g <= 1 and g + 1 < groups:
            pack(g + 1)
            begin(g + 1)
        if k == min(2, last) and g >= 1 and g + 2 < groups:
            pack(g + 2)
            begin(g + 2)
        if k == 1 and g + 1 < groups:
            share(g + 1, owns[g + 1], place)

        @pl.when(place >= k)
        def _():
            share(g, from_left[g * (line - 1) + k - 1], place - k)

        @pl.when(place + k <= last)
        def _():
            share(g, from_right[g * (line - 1) + k - 1], place + k)

    def wait_chosen(g):
        def one(d):
            def source(i, _):
                plane_copy(g, d, i).wait_recv()
                return 0

            lax.fori_loop(0, line, source, 0)

        over_peers(one)

    over_peers(lambda d: ask_copy(d).start())
    begin(0)
    over_peers(lambda d: ask_copy(d).wait_recv())
    to_smem = pltpu.make_async_copy(asked, asked_smem, local_sem.at[1])
    to_smem.start()
    to_smem.wait()
    share(0, owns[0], place)
    for k in range(1, line):
        hop(0, k)
    q_copy.wait()

    scale = math.log2(math.e) / math.sqrt(HEAD_SIZE)
    first_block = lax.rem(part + 1, parts) * part_rows // BLOCK_TOKENS

    def out_remote(g, index, piece):
        target = index // part_chunks
        row = pl.multiple_of(lax.rem(index, part_chunks) * chunk, chunk)
        col = pl.multiple_of(part * cols + g * width + piece * piece_cols, HEAD_SIZE)
        src_row = pl.multiple_of(index * chunk, chunk)
        src_col = pl.multiple_of(g * width + piece * piece_cols, HEAD_SIZE)
        src = o_ref.at[pl.ds(src_row, chunk), pl.ds(src_col, piece_cols)]
        dst = out_ref.at[pl.ds(row, chunk), pl.ds(col, piece_cols)]
        slot = part * part_chunks + lax.rem(index, part_chunks)
        remote = pltpu.make_async_remote_copy(
            src_ref=src,
            dst_ref=dst,
            send_sem=out_send.at[g, index, piece],
            recv_sem=out_recv.at[g, slot, piece],
            device_id=(me, target),
            device_id_type=MESH,
        )
        local = pltpu.make_async_copy(src, dst, out_send.at[g, index, piece])
        return target, remote, local

    hop_turn = {k: (k - 1) * blocks // (line - 1) + (1 if k > 1 else 0) for k in range(1, line)}
    hop_turn = {k: min(turn, blocks - 1) for k, turn in hop_turn.items()}

    def step(t, _):
        g = t // blocks
        turn = lax.rem(t, blocks)
        b = lax.rem(first_block + turn, blocks)
        for gi in range(groups):
            for ti in range(blocks):
                hops = [k for k in range(1, line) if hop_turn[k] == ti and gi + 1 < groups]
                if not hops and ti > 0:
                    continue

                @pl.when(jnp.logical_and(g == gi, turn == ti))
                def _():
                    for k in hops:
                        hop(gi + 1, k)
                    if ti == 0:
                        wait_chosen(gi)

            @pl.when(g == gi)
            def _():
                k_sel[:, :BLOCK_TOKENS] = owns[gi][b, :HEAD_SIZE, :]
                v_sel[:BLOCK_TOKENS, :HEAD_SIZE] = owns[gi][b, HEAD_SIZE:, :]
                for j in range(1, picked):
                    owner = picks_ref[b, j] // blocks
                    slot = lax.rem(lax.rem(owner, plane) + (plane - 1) - seat + plane, plane)
                    rows = slice(j * BLOCK_TOKENS, (j + 1) * BLOCK_TOKENS)
                    k_sel[:, rows] = chosen[gi][slot, owner // plane, :HEAD_SIZE, :]
                    v_sel[rows, :HEAD_SIZE] = chosen[gi][slot, owner // plane, HEAD_SIZE:, :]

        q_rows = pl.ds(pl.multiple_of(b * BLOCK_TOKENS, BLOCK_TOKENS), BLOCK_TOKENS)
        row_id = lax.broadcasted_iota(jnp.int32, (pair * BLOCK_TOKENS, BLOCK_TOKENS), 0)
        key_id = lax.broadcasted_iota(jnp.int32, (pair * BLOCK_TOKENS, BLOCK_TOKENS), 1)
        causal = key_id <= lax.rem(row_id, BLOCK_TOKENS)
        span = picked * BLOCK_TOKENS
        tile = 2 * BLOCK_TOKENS if span % (2 * BLOCK_TOKENS) == 0 else BLOCK_TOKENS

        def lanes_of(h):
            start = pl.multiple_of(g * width + h * HEAD_SIZE, HEAD_SIZE)
            return pl.ds(start, HEAD_SIZE)

        def load_queries(h):
            return jnp.concatenate([q_ref[q_rows, lanes_of(h + u)] for u in range(pair)], axis=0)

        def score_tile(q, start):
            keys = k_sel[:, start : start + tile]
            scores = jnp.dot(q, keys, preferred_element_type=jnp.float32)
            if start == 0:
                own = jnp.where(causal, scores[:, :BLOCK_TOKENS], -jnp.inf)
                scores = jnp.concatenate([own, scores[:, BLOCK_TOKENS:]], axis=1)
            return scores

        def send_out(piece):
            for c in range(block_chunks):
                target, remote, local = out_remote(g, b * block_chunks + c, piece)

                @pl.when(target != part)
                def _():
                    remote.start()

                @pl.when(target == part)
                def _():
                    local.start()

        starts = range(0, span, tile)
        q = load_queries(0)
        tiles = [score_tile(q, start) for start in starts]
        for h in range(0, heads, pair):
            top = functools.reduce(jnp.maximum, tiles)
            top = jnp.max(top, axis=1, keepdims=True)
            more = h + pair < heads
            if more:
                q = load_queries(h + pair)
            weights, following = [], []
            for scores, start in zip(tiles, starts):
                if more:
                    following.append(score_tile(q, start))
                weights.append(jnp.exp2((scores - top) * scale).astype(jnp.bfloat16))
            weights = jnp.concatenate(weights, axis=1)
            both = jnp.dot(weights, v_sel[...], preferred_element_type=jnp.float32)
            result = (both[:, :HEAD_SIZE] / both[:, HEAD_SIZE:]).astype(jnp.bfloat16)
            for u in range(pair):
                o_ref[q_rows, lanes_of(h + u)] = result[u * BLOCK_TOKENS : (u + 1) * BLOCK_TOKENS]
            tiles = following
            done = (h + pair) * HEAD_SIZE
            if done % piece_cols == 0:
                send_out(done // piece_cols - 1)
        return 0

    lax.fori_loop(0, groups * blocks, step, 0)

    def finish(t, _):
        g = t // (parts * part_chunks * pieces)
        index = lax.rem(t // pieces, parts * part_chunks)
        piece = lax.rem(t, pieces)
        target, remote, local = out_remote(g, index, piece)

        @pl.when(target != part)
        def _():
            remote.wait_send()
            row = pl.multiple_of(lax.rem(index, part_chunks) * chunk, chunk)
            col = pl.multiple_of(target * cols + g * width + piece * piece_cols, HEAD_SIZE)
            landed = out_ref.at[pl.ds(row, chunk), pl.ds(col, piece_cols)]
            pltpu.make_async_remote_copy(
                src_ref=landed,
                dst_ref=landed,
                send_sem=out_send.at[g, index, piece],
                recv_sem=out_recv.at[g, index, piece],
                device_id=(me, target),
                device_id_type=MESH,
            ).wait_recv()

        @pl.when(target == part)
        def _():
            local.wait()

        return 0

    def plane_done(d):
        for g in range(groups):

            def source(i, _):
                plane_copy(g, d, i).wait_send()
                return 0

            lax.fori_loop(0, line, source, 0)

    over_peers(lambda d: ask_copy(d).wait_send())
    over_peers(plane_done)
    for g in range(groups):
        for k in range(line - 1):

            @pl.when(jnp.logical_and(place < line - 1, place >= k))
            def _():
                for i in range(blocks):
                    right_copy(g, k, i).wait_send()

            @pl.when(jnp.logical_and(place > 0, place + k <= line - 1))
            def _():
                for i in range(blocks):
                    left_copy(g, k, i).wait_send()

    lax.fori_loop(0, groups * parts * part_chunks * pieces, finish, 0)


def body(line, queries, key_vector_rows, value_vector_rows, block_picks):
    n = lax.axis_size("ctx")
    parts = lax.axis_size("kvh")
    tokens, cols = queries.shape
    blocks = tokens // BLOCK_TOKENS
    picked = block_picks.shape[1]
    groups = key_vector_rows.shape[1] // HEAD_SIZE
    width = cols // groups
    keys = key_vector_rows.reshape(blocks, BLOCK_TOKENS, groups * HEAD_SIZE)
    values = value_vector_rows.reshape(blocks, BLOCK_TOKENS, groups * HEAD_SIZE)
    owned = (block_picks // blocks)[None] == jnp.arange(n, dtype=jnp.int32)[:, None, None]
    wanted = jnp.max(jnp.where(owned, (block_picks % blocks)[None], 0), axis=(1, 2))
    lanes = -(-n // 128) * 128
    wanted = jnp.pad(wanted, (0, lanes - n)).reshape(1, lanes)

    vmem = pl.BlockSpec(memory_space=pltpu.VMEM)
    anywhere = pl.BlockSpec(memory_space=pl.ANY)
    hbm = pl.BlockSpec(memory_space=pltpu.HBM)
    part_rows = tokens // parts
    chunks = tokens // min(BLOCK_TOKENS, part_rows)
    plane = n // line
    shard = pltpu.VMEM((blocks, 2 * BLOCK_TOKENS, HEAD_SIZE), jnp.bfloat16)
    stage = pltpu.VMEM((plane - 1, line, 2 * BLOCK_TOKENS, HEAD_SIZE), jnp.bfloat16)
    slots = pltpu.VMEM((plane, line, 2 * BLOCK_TOKENS, HEAD_SIZE), jnp.bfloat16)
    return pl.pallas_call(
        functools.partial(attend_kernel, n, line, parts, groups, blocks, picked, width),
        out_shape=jax.ShapeDtypeStruct((part_rows, parts * cols), jnp.bfloat16),
        in_specs=[vmem, pl.BlockSpec(memory_space=pltpu.SMEM), hbm, hbm, hbm],
        out_specs=anywhere,
        scratch_shapes=[shard] * (groups * (2 * line - 1))
        + [stage] * groups
        + [slots] * groups
        + [
            pltpu.VMEM((plane, 1, lanes), jnp.int32),
            pltpu.SMEM((plane, 1, lanes), jnp.int32),
            pltpu.VMEM((tokens, cols), jnp.bfloat16),
            pltpu.VMEM(keys.shape, jnp.bfloat16),
            pltpu.VMEM(values.shape, jnp.bfloat16),
            pltpu.VMEM((tokens, cols), jnp.bfloat16),
            pltpu.VMEM((HEAD_SIZE, picked * BLOCK_TOKENS), jnp.bfloat16),
            pltpu.VMEM((picked * BLOCK_TOKENS, 2 * HEAD_SIZE), jnp.bfloat16),
            pltpu.SemaphoreType.DMA((plane - 1,)),
            pltpu.SemaphoreType.DMA((plane - 1,)),
            pltpu.SemaphoreType.DMA((groups, line, blocks)),
            pltpu.SemaphoreType.DMA((groups, line, blocks)),
            pltpu.SemaphoreType.DMA((groups, line, blocks)),
            pltpu.SemaphoreType.DMA((groups, line, blocks)),
            pltpu.SemaphoreType.DMA((groups, plane - 1, line)),
            pltpu.SemaphoreType.DMA((groups, plane - 1, line)),
            pltpu.SemaphoreType.DMA((groups, chunks, 2)),
            pltpu.SemaphoreType.DMA((groups, chunks, 2)),
            pltpu.SemaphoreType.DMA((4,)),
        ],
        compiler_params=pltpu.CompilerParams(
            collective_id=0, has_side_effects=True, vmem_limit_bytes=48 * 2**20
        ),
        cost_estimate=pl.CostEstimate(
            flops=4 * tokens * cols * picked * BLOCK_TOKENS,
            bytes_accessed=4 * tokens * cols,
            transcendentals=tokens * (cols // HEAD_SIZE) * picked * BLOCK_TOKENS,
        ),
    )(wanted, block_picks, queries, keys, values)


def line_length(mesh):
    n = mesh.shape["ctx"]
    column = mesh.devices.reshape(n, -1)[:, 0]
    places = [getattr(device, "coords", None) for device in column]
    if places[0] is not None:
        firsts = [
            next((i for i in range(n) if places[i][axis] != places[0][axis]), 0)
            for axis in range(len(places[0]))
        ]
        if 1 < max(firsts) < n and n % max(firsts) == 0:
            return n // max(firsts)
    return next(a for a in range(math.isqrt(n), 0, -1) if n % a == 0)


def solution(mesh):
    return jax.shard_map(
        functools.partial(body, line_length(mesh)),
        mesh=mesh,
        in_specs=(P("ctx", "kvh"), P("ctx", "kvh"), P("ctx", "kvh"), P("ctx", None)),
        out_specs=P(("ctx", "kvh"), None),
        check_vma=False,
    )
```
